128 devices in a mesh: section: 16 (over x_hi, y, core), dp: 8 (over z, x_lo).
Axes of the slice: x: 4 (x_hi: 2, x_lo: 2; x = x_hi * 2 + x_lo), y: 4, z: 4, core: 2. Of those that a mesh axis runs over, the one named last changes fastest.
Arguments:
- tokens: bfloat16 [32768, 4096], P(('section', 'dp')), may hold values from -6 to 6
- norm_gain: float32 [4096], replicated, may hold values from 0.1 to 1.9
- gate_weight: bfloat16 [4096, 8192], P(None, 'section'), may hold values from -0.09375 to 0.09375
- up_weight: bfloat16 [4096, 8192], P(None, 'section'), may hold values from -0.09375 to 0.09375
- down_weight: bfloat16 [8192, 4096], P('section'), may hold values from -0.1875 to 0.1875
- cotangent: bfloat16 [32768, 4096], P(('section', 'dp')), may hold values from -24 to 24
Outputs:
- layer_out: bfloat16 [32768, 4096], P(('section', 'dp'))
- input_grad: bfloat16 [32768, 4096], P(('section', 'dp'))
- gate_grad: float32 [4096, 8192], P('dp', 'section')
- up_grad: float32 [4096, 8192], P('dp', 'section')
- down_grad: float32 [8192, 4096], P('section', 'dp')
The draws below stay inside these ranges and needn't reach their ends.
All inputs are finite; a program needn't handle non-finite values.
Results may differ from the reference program's by a relative error of at most 0.018.
Values may be sent and summed in bfloat16 or wider, within the bound.
A program may use at most 192 MiB of HBM per device.

```python
import jax
import jax.numpy as jnp
from jax import lax

D = 4096
FF_BLK = 512
TOK = 256
ROUNDS = 2
FF = 8192
TOKENS = 32768
N_SECTION = 16
N_DP = 8


def with_spikes(result, rng, source, target, blocks, factor):
    def block_of(axis_at):
        return (jnp.arange(result.shape[axis_at]) // (result.shape[axis_at] // blocks)).reshape((-1,) + (1,) * (result.ndim - 1 - axis_at))

    one_side = jax.random.permutation(rng, blocks)[block_of(target)]
    second = (block_of(target) + blocks // 2) % blocks
    return jnp.where((block_of(source) == one_side) | (block_of(source) == second), factor * result, result)


def level_of(stream_key, shape, cuts, least, largest):
    level = 1.0
    for axis_at, blocks in cuts:
        draws = jax.random.uniform(jax.random.fold_in(jax.random.fold_in(stream_key, 6), axis_at), (blocks,), jnp.float32, least / len(cuts), largest / len(cuts))
        level = level * jnp.repeat(jnp.exp(draws), shape[axis_at] // blocks).reshape((-1,) + (1,) * (len(shape) - 1 - axis_at))
    return level


def gaussian(rng, extent, scale, bound, split=(), kind=jnp.bfloat16):
    values = scale * jax.random.normal(rng, extent, jnp.float32)
    if split:
        values = values * level_of(rng, extent, split, -0.22, 0.18)
    return jnp.clip(values, -bound, bound).astype(kind)


def bell_draw_with(stream_key, extent, deviation, bound, pieces, heavy, dtype=jnp.bfloat16):
    values = deviation * jax.random.normal(stream_key, extent, jnp.float32)
    if pieces:
        values = values * level_of(stream_key, extent, pieces, -0.22, 0.18)
    return jnp.clip(with_spikes(values, jax.random.fold_in(stream_key, 3), *heavy), -bound, bound).astype(dtype)


def setup_inputs(seed: int = 0) -> dict:
    splits = jax.random.split(jax.random.key(seed), 7)
    return {
        "tokens": gaussian(splits[0], (TOKENS, D), 1.0, 6.0, ((0, 128),)),
        "norm_gain": jnp.clip(1.0 + 0.18 * jax.random.normal(splits[1], (D,), jnp.float32), 0.1, 1.9),
        "gate_weight": gaussian(splits[2], (D, FF), D ** -0.5, 0.09375, ((1, 16),)),
        "up_weight": gaussian(splits[3], (D, FF), D ** -0.5, 0.09375, ((1, 16),)),
        "down_weight": gaussian(splits[4], (FF, D), (ROUNDS * FF_BLK) ** -0.5, 0.1875, ((0, 16),)),
        "cotangent": bell_draw_with(splits[5], (TOKENS, D), 1.0, 24.0, ((0, 128),), (0, 1, 128, 5.5)),
    }


def block_terms(normed, grad_out, weight_gate, weight_up, weight_down):
    gate_act = jnp.dot(normed, weight_gate, preferred_element_type=jnp.float32)
    up_act = jnp.dot(normed, weight_up, preferred_element_type=jnp.float32)
    sigmoid_gate = jax.nn.sigmoid(gate_act)
    swish_gate = gate_act * sigmoid_gate
    hidden = (swish_gate * up_act).astype(jnp.bfloat16)
    partial_out = jnp.dot(hidden, weight_down, preferred_element_type=jnp.float32)
    grad_hidden = jnp.dot(grad_out, weight_down.T, preferred_element_type=jnp.float32)
    grad_gate = (grad_hidden * up_act * sigmoid_gate * (1.0 + gate_act * (1.0 - sigmoid_gate))).astype(jnp.bfloat16)
    grad_up = (grad_hidden * swish_gate).astype(jnp.bfloat16)
    grad_normed = jnp.dot(grad_gate, weight_gate.T, preferred_element_type=jnp.float32)
    grad_normed = grad_normed + jnp.dot(grad_up, weight_up.T, preferred_element_type=jnp.float32)
    term_gate = jnp.dot(normed.T, grad_gate, preferred_element_type=jnp.float32)
    term_up = jnp.dot(normed.T, grad_up, preferred_element_type=jnp.float32)
    term_down = jnp.dot(hidden.T, grad_out, preferred_element_type=jnp.float32)
    return (partial_out, grad_normed, term_gate, term_up, term_down)

def reference(tokens, norm_gain, gate_weight, up_weight, down_weight, cotangent):
    group_rows = N_DP * TOK
    token_groups = tokens.reshape(N_SECTION, group_rows, D)
    grad_groups = cotangent.reshape(N_SECTION, group_rows, D)
    gate_blocks = gate_weight.reshape(D, N_SECTION, FF_BLK).transpose(1, 0, 2)
    up_blocks = up_weight.reshape(D, N_SECTION, FF_BLK).transpose(1, 0, 2)
    down_blocks = down_weight.reshape(N_SECTION, FF_BLK, D)
    gate_met = jnp.stack([jnp.roll(gate_blocks, offset, axis=0) for offset in range(ROUNDS)], axis=1)
    up_met = jnp.stack([jnp.roll(up_blocks, offset, axis=0) for offset in range(ROUNDS)], axis=1)
    down_met = jnp.stack([jnp.roll(down_blocks, offset, axis=0) for offset in range(ROUNDS)], axis=1)
    gain_float = norm_gain.astype(jnp.float32)

    def section_pass(inputs):
        group_tokens, group_grad, gates, ups, downs = inputs
        values = group_tokens.astype(jnp.float32)
        inverse = lax.rsqrt(lax.optimization_barrier(jnp.mean(values * values, axis=1, keepdims=True)) + 1e-05)
        normed = (values * inverse * gain_float).astype(jnp.bfloat16)
        totals = values
        grad_sum = jnp.zeros_like(values)
        gate_terms, up_terms, down_terms = ([], [], [])
        for offset in range(ROUNDS):
            partial_out, grad_normed, term_gate, term_up, term_down = block_terms(normed, group_grad, gates[offset], ups[offset], downs[offset])
            totals = totals + partial_out
            grad_sum = grad_sum + grad_normed
            gate_terms.append(term_gate)
            up_terms.append(term_up)
            down_terms.append(term_down)
        scaled = grad_sum * gain_float
        mixed = lax.optimization_barrier(jnp.mean(scaled * values, axis=1, keepdims=True))
        input_grad = group_grad.astype(jnp.float32) + inverse * scaled - values * inverse ** 3 * mixed
        return (totals.astype(jnp.bfloat16), input_grad.astype(jnp.bfloat16), jnp.stack(gate_terms), jnp.stack(up_terms), jnp.stack(down_terms))
    layer_out, input_grad, gate_terms, up_terms, down_terms = lax.map(section_pass, (token_groups, grad_groups, gate_met, up_met, down_met))
    factor = 1.0 / jnp.sqrt(jnp.float32(ROUNDS * N_DP * TOK))
    gate_sum = sum((jnp.roll(gate_terms[:, offset], -offset, axis=0) for offset in range(ROUNDS))) * factor
    up_sum = sum((jnp.roll(up_terms[:, offset], -offset, axis=0) for offset in range(ROUNDS))) * factor
    down_sum = sum((jnp.roll(down_terms[:, offset], -offset, axis=0) for offset in range(ROUNDS))) * factor
    gate_grad = gate_sum.transpose(1, 0, 2).reshape(D, N_SECTION * FF_BLK)
    up_grad = up_sum.transpose(1, 0, 2).reshape(D, N_SECTION * FF_BLK)
    down_grad = down_sum.reshape(N_SECTION * FF_BLK, D)
    return (layer_out.reshape(N_SECTION * group_rows, D), input_grad.reshape(N_SECTION * group_rows, D), gate_grad, up_grad, down_grad)
```

```python
import math

import jax
import jax.numpy as jnp
from jax import lax
from jax.sharding import PartitionSpec as P

ROUNDS = 2


def from_behind(array, axis, by):
    peers = lax.axis_size(axis)
    return lax.ppermute(array, axis, [(i, (i + by) % peers) for i in range(peers)])


def acts(normed, grad_out, weight_gate, weight_up, weight_down):
    gate_act = jnp.dot(normed, weight_gate, preferred_element_type=jnp.float32)
    up_act = jnp.dot(normed, weight_up, preferred_element_type=jnp.float32)
    sigmoid_gate = jax.nn.sigmoid(gate_act)
    swish_gate = gate_act * sigmoid_gate
    hidden = (swish_gate * up_act).astype(jnp.bfloat16)
    partial_out = jnp.dot(hidden, weight_down, preferred_element_type=jnp.float32)
    grad_hidden = jnp.einsum("td,fd->tf", grad_out, weight_down, preferred_element_type=jnp.float32)
    grad_gate = (
        grad_hidden * up_act * sigmoid_gate * (1.0 + gate_act * (1.0 - sigmoid_gate))
    ).astype(jnp.bfloat16)
    grad_up = (grad_hidden * swish_gate).astype(jnp.bfloat16)
    grad_normed = jnp.einsum(
        "tf,df->td", grad_gate, weight_gate, preferred_element_type=jnp.float32
    )
    grad_normed = grad_normed + jnp.einsum(
        "tf,df->td", grad_up, weight_up, preferred_element_type=jnp.float32
    )
    return partial_out, grad_normed, hidden, grad_gate, grad_up


def group_sum(term, axis):
    return lax.psum_scatter(
        term.astype(jnp.bfloat16), "dp", scatter_dimension=axis, tiled=True
    ).astype(jnp.float32)


def normalize(tokens, norm_gain):
    values = tokens.astype(jnp.float32)
    inverse = lax.rsqrt(jnp.mean(values * values, axis=1, keepdims=True) + 1e-05)
    return values, inverse, (values * inverse * norm_gain).astype(jnp.bfloat16)


def body(tokens, norm_gain, gate_weight, up_weight, down_weight, cotangent):
    rows = tokens.shape[0]
    factor = 1.0 / math.sqrt(ROUNDS * lax.axis_size("dp") * rows)
    next_tokens, next_cotangent = from_behind((tokens, cotangent), "section", -1)
    values, inverse, normed = normalize(tokens, norm_gain)
    weights = (gate_weight, up_weight, down_weight)
    out_a, grad_a, hidden_a, gg_a, gu_a = acts(normed, cotangent, *weights)
    _, _, next_normed = normalize(next_tokens, norm_gain)
    out_b, grad_b, hidden_b, gg_b, gu_b = acts(next_normed, next_cotangent, *weights)
    back_out, back_grad = from_behind(
        (out_b.astype(jnp.bfloat16), grad_b.astype(jnp.bfloat16)), "section", 1
    )
    all_normed = jnp.concatenate([normed, next_normed])
    all_cot = jnp.concatenate([cotangent, next_cotangent])

    def outer(a, b):
        return jnp.einsum("td,tf->df", a, b, preferred_element_type=jnp.float32) * factor

    down = group_sum(outer(jnp.concatenate([hidden_a, hidden_b]), all_cot), 1)
    gate = group_sum(outer(all_normed, jnp.concatenate([gg_a, gg_b])), 0)
    up = group_sum(outer(all_normed, jnp.concatenate([gu_a, gu_b])), 0)
    totals = values + (out_a + back_out.astype(jnp.float32))
    scaled = (grad_a + back_grad.astype(jnp.float32)) * norm_gain
    mixed = jnp.mean(scaled * values, axis=1, keepdims=True)
    input_grad = cotangent.astype(jnp.float32) + inverse * scaled - values * inverse**3 * mixed
    return (totals.astype(jnp.bfloat16), input_grad.astype(jnp.bfloat16), gate, up, down)


def solution(mesh):
    in_specs = (
        P(("section", "dp"), None),
        P(),
        P(None, "section"),
        P(None, "section"),
        P("section", None),
        P(("section", "dp"), None),
    )
    out_specs = (
        P(("section", "dp"), None),
        P(("section", "dp"), None),
        P("dp", "section"),
        P("dp", "section"),
        P("section", "dp"),
    )
    return jax.shard_map(body, mesh=mesh, in_specs=in_specs, out_specs=out_specs, check_vma=False)
```

```python
import functools
import math

import jax
import jax.numpy as jnp
from jax import lax
from jax.experimental import pallas as pl
from jax.experimental.pallas import tpu as pltpu
from jax.sharding import PartitionSpec as P

ROUNDS = 2
GATE, UP, DOWN = 0, 1, 2
MESH = pl.DeviceIdType.MESH
F32 = jnp.float32
BF16 = jnp.bfloat16


def dot_nt(a, b):
    return lax.dot_general(a, b, (((1,), (1,)), ((), ())), preferred_element_type=F32)


def kernel(
    sections,
    tokens,
    gain_hbm,
    gate_hbm,
    up_hbm,
    down_hbm,
    cotangent,
    layer_out,
    input_grad,
    gate_grad,
    up_grad,
    down_grad,
    gain,
    weight_in,
    weight_down,
    tok,
    normed,
    cot,
    inverse,
    gate_act,
    up_act,
    acts,
    acts_t,
    scaled,
    back_out,
    back_grad,
    ret_out,
    ret_grad,
    a1_out,
    a1_in,
    a2_out,
    a2_in,
    ax_in,
    bx_out,
    bx_in,
    bz1_in,
    bz2_in,
    result,
    load_sem,
    store_sem,
    tok_sem,
    back_sem,
    a1_sem,
    a2_sem,
    ax_sem,
    bx_sem,
    bz1_sem,
    bz2_sem,
):
    rows, depth = tok.shape
    ff = weight_down.shape[0]
    half = ff // 2
    piece = depth // 8
    factor = 1.0 / math.sqrt(ROUNDS * 8 * rows)

    s = lax.axis_index("section")
    j = lax.axis_index("dp")
    core = lax.rem(s, 2)
    z, xl = j // 2, lax.rem(j, 2)
    mirrored = j + 1 - 2 * xl
    before, after = lax.rem(s + sections - 1, sections), lax.rem(s + 1, sections)
    j_before = jnp.where(lax.rem(s, 8) == 0, mirrored, j)
    j_after = jnp.where(lax.rem(after, 8) == 0, mirrored, j)
    to_before, to_after = (before, j_before), (after, j_after)
    partner = (s, mirrored)

    def plane(by):
        return lax.rem(z + by, 4)

    def neighbour(way):
        return (s, plane(1 + 2 * way) * 2 + xl)

    def remote(src, dst, sems, device):
        return pltpu.make_async_remote_copy(
            src_ref=src,
            dst_ref=dst,
            send_sem=sems.at[0],
            recv_sem=sems.at[1],
            device_id=device,
            device_id_type=MESH,
        )

    loads = [
        pltpu.make_async_copy(src, dst, load_sem.at[i])
        for i, (src, dst) in enumerate(
            (
                (tokens, tok),
                (gain_hbm, gain),
                (gate_hbm, weight_in.at[GATE]),
                (up_hbm, weight_in.at[UP]),
                (cotangent, cot.at[pl.ds(0, rows)]),
                (down_hbm, weight_down),
            )
        )
    ]
    for load in loads:
        load.start()

    barrier = pltpu.get_barrier_semaphore()
    for device in (to_before, to_after, partner, neighbour(0), neighbour(1)):
        pl.semaphore_signal(barrier, inc=1, device_id=device, device_id_type=MESH)
    pl.semaphore_wait(barrier, 5)

    send_tok = remote(tokens, normed.at[pl.ds(rows, rows)], tok_sem.at[0], to_before)
    send_cot = remote(cotangent, cot.at[pl.ds(rows, rows)], tok_sem.at[1], to_before)
    send_out = remote(back_out, ret_out, back_sem.at[0], to_after)
    send_grad = remote(back_grad, ret_grad, back_sem.at[1], to_after)
    send_tok.start()
    send_cot.start()

    def normalize(src, first, keep):
        def step(i, _):
            at = pl.ds(pl.multiple_of(i * 16, 16), 16)
            to = pl.ds(pl.multiple_of(first + i * 16, 16), 16)
            values = (src[at] if keep else src[to]).astype(F32)
            inv = lax.rsqrt(jnp.sum(values * values, axis=1, keepdims=True) / depth + 1e-05)
            if keep:
                inverse[at] = jnp.broadcast_to(inv, (16, 128))
            normed[to] = (values * inv * gain[...]).astype(BF16)
            return 0

        lax.fori_loop(0, rows // 16, step, 0)

    def forward(first):
        here = pl.ds(first, rows)

        def step(h, _):
            cols = pl.ds(pl.multiple_of(h * half, half), half)
            g = jnp.dot(normed[here], weight_in[GATE, :, cols], preferred_element_type=F32)
            u = jnp.dot(normed[here], weight_in[UP, :, cols], preferred_element_type=F32)
            gate_act[:, cols] = g
            up_act[:, cols] = u
            hidden = g * jax.nn.sigmoid(g) * u
            acts[DOWN, here, cols] = hidden.astype(BF16)
            acts_t[DOWN, cols, here] = hidden.T.astype(BF16)
            return 0

        lax.fori_loop(0, 2, step, 0)

    def backward(first):
        here = pl.ds(first, rows)

        def step(h, _):
            cols = pl.ds(pl.multiple_of(h * half, half), half)
            grad_hidden = dot_nt(cot[here], weight_down[cols])
            g, u = gate_act[:, cols], up_act[:, cols]
            sig = jax.nn.sigmoid(g)
            grad_gate = grad_hidden * u * sig * (1.0 + g * (1.0 - sig))
            grad_up = grad_hidden * (g * sig)
            acts[GATE, here, cols] = grad_gate.astype(BF16)
            acts[UP, here, cols] = grad_up.astype(BF16)
            acts_t[GATE, cols, here] = grad_gate.T.astype(BF16)
            acts_t[UP, cols, here] = grad_up.T.astype(BF16)
            return 0

        lax.fori_loop(0, 2, step, 0)

    def chunk(c):
        return pl.ds(pl.multiple_of(c * piece, piece), piece)

    def out_chunk(first, c):
        return jnp.dot(
            acts[DOWN, pl.ds(first, rows)], weight_down[:, chunk(c)], preferred_element_type=F32
        )

    def grad_chunk(first, c):
        here = pl.ds(first, rows)
        return dot_nt(acts[GATE, here], weight_in[GATE, chunk(c)]) + dot_nt(
            acts[UP, here], weight_in[UP, chunk(c)]
        )

    def return_out():
        def step(c, _):
            back_out[:, chunk(c)] = out_chunk(rows, c).astype(BF16)
            return 0

        lax.fori_loop(0, 8, step, 0)
        send_out.start()

    def return_grad():
        def step(c, _):
            back_grad[:, chunk(c)] = grad_chunk(rows, c).astype(BF16)
            return 0

        lax.fori_loop(0, 8, step, 0)
        send_grad.start()

    store_out = pltpu.make_async_copy(ret_out, layer_out, store_sem.at[0])
    store_grad = pltpu.make_async_copy(ret_grad, input_grad, store_sem.at[1])

    def finish_rows():
        send_out.wait_recv()

        def out_step(c, _):
            at = chunk(c)
            total = tok[:, at].astype(F32) + out_chunk(0, c) + ret_out[:, at].astype(F32)
            ret_out[:, at] = total.astype(BF16)
            return 0

        lax.fori_loop(0, 8, out_step, 0)
        store_out.start()
        send_grad.wait_recv()

        def grad_step(c, mixed):
            at = chunk(c)
            g = (grad_chunk(0, c) + ret_grad[:, at].astype(F32)) * gain[:, at]
            scaled[:, at] = g
            return mixed + jnp.sum(g * tok[:, at].astype(F32), axis=1, keepdims=True)

        mixed = lax.fori_loop(0, 8, grad_step, jnp.zeros((rows, 1), F32))
        inv = inverse[:, :1]
        weight = inv * inv * inv * (mixed / depth)

        def last_step(c, _):
            at = chunk(c)
            total = cot[pl.ds(0, rows), at].astype(F32) + inv * scaled[:, at]
            total = total - tok[:, at].astype(F32) * weight
            ret_grad[:, at] = total.astype(BF16)
            return 0

        lax.fori_loop(0, 8, last_step, 0)
        store_grad.start()

    def tile(which, x, to_plane, to_x, out_rows, put, adds):
        first = (to_plane * 2 + to_x) * piece
        for c in range(2):
            at = pl.ds(c * (piece // 2), piece // 2)
            cols = pl.ds(pl.multiple_of(first + c * (piece // 2), piece // 2), piece // 2)
            acc = jnp.dot(acts_t[which, out_rows], x[:, cols], preferred_element_type=F32)
            for ref in adds:
                acc = acc + ref[:, at].astype(F32)
            put(at, acc)

    def into(ref):
        def put(at, acc):
            ref[:, at] = acc.astype(BF16)

        return put

    whole = pl.ds(0, ff)

    def half_rows(h):
        return pl.ds(pl.multiple_of(h * half, half), half)

    def copy_a1(m, way):
        return remote(a1_out.at[m, way], a1_in.at[m, way], a1_sem.at[m, way], neighbour(way))

    def copy_a2(m, way, merged):
        src = a1_in.at[m, way] if merged else a2_out.at[m, way]
        return remote(
            src, a2_in.at[m, way, merged], a2_sem.at[m, way, merged], neighbour(way)
        )

    def copy_ax(m):
        return remote(a2_in.at[m, 0, xl], ax_in.at[m], ax_sem.at[m], partner)

    def copy_bx(k):
        return remote(bx_out.at[k], bx_in.at[k], bx_sem.at[k], partner)

    def copy_bz1(way):
        return remote(
            bx_in.at[0, half_rows(way)], bz1_in.at[way], bz1_sem.at[way], neighbour(way)
        )

    def copy_bz2(way, merged):
        part = way if merged else 1 - way
        return remote(
            bx_in.at[1 + way, half_rows(part)],
            bz2_in.at[way, merged],
            bz2_sem.at[way, merged],
            neighbour(way),
        )

    def a1_step(m):
        def step(way, _):
            tile(m, normed, plane(2), way, whole, into(a1_out.at[m, way]), ())
            copy_a1(m, way).start()
            return 0

        lax.fori_loop(0, 2, step, 0)

    def bx_step(k):
        by = (2, 1, 3, 0)[k]
        tile(DOWN, cot, plane(by), 1 - xl, whole, into(bx_out.at[k]), ())
        copy_bx(k).start()

    def a2_direct(m):
        def step(way, _):
            tile(m, normed, plane(1 + 2 * way), 1 - way, whole, into(a2_out.at[m, way]), ())
            copy_a2(m, way, 0).start()
            return 0

        lax.fori_loop(0, 2, step, 0)

    def a2_merged(m):
        def step(way, _):
            copy_a1(m, way).wait_recv()
            here = a1_in.at[m, way]
            tile(m, normed, plane(1 + 2 * way), way, whole, into(here), (here,))
            copy_a2(m, way, 1).start()
            return 0

        lax.fori_loop(0, 2, step, 0)

    def b_opposite():
        copy_bx(0).wait_recv()
        here = bx_in.at[0]
        tile(DOWN, cot, plane(2), xl, whole, into(here), (here,))
        copy_bz1(0).start()
        copy_bz1(1).start()

    def b_direct():
        def step(way, _):
            copy_bx(1 + way).wait_recv()
            part = half_rows(1 - way)
            here = bx_in.at[1 + way, part]
            tile(DOWN, cot, plane(1 + 2 * way), xl, part, into(here), (here,))
            copy_bz2(way, 0).start()
            return 0

        lax.fori_loop(0, 2, step, 0)

    def b_merged():
        def step(way, _):
            copy_bz1(way).wait_recv()
            part = half_rows(way)
            here = bx_in.at[1 + way, part]
            tile(DOWN, cot, plane(1 + 2 * way), xl, part, into(here), (here, bz1_in.at[way]))
            copy_bz2(way, 1).start()
            return 0

        lax.fori_loop(0, 2, step, 0)

    def a_cross(m):
        for way in range(2):
            for merged in range(2):
                copy_a2(m, way, merged).wait_recv()
        here = a2_in.at[m, 0, xl]
        tile(m, normed, z, 1 - xl, whole, into(here), (here, a2_in.at[m, 1, 1 - xl]))
        copy_ax(m).start()

    def a_last(m, out, sem):
        copy_ax(m).wait_recv()

        def put(at, acc):
            result[m, at, :] = (acc * factor).T

        adds = (a2_in.at[m, 0, 1 - xl], a2_in.at[m, 1, xl], ax_in.at[m])
        tile(m, normed, z, xl, whole, put, adds)
        copy = pltpu.make_async_copy(result.at[m], out, sem)
        copy.start()
        return copy

    def b_last(out, sem):
        copy_bx(3).wait_recv()
        for way in range(2):
            for merged in range(2):
                copy_bz2(way, merged).wait_recv()

        def step(h, _):
            part = half_rows(h)

            def put(at, acc):
                result[DOWN, part, at] = acc * factor

            adds = (bx_in.at[3, part], bz2_in.at[0, 1 - h], bz2_in.at[1, h])
            tile(DOWN, cot, z, xl, part, put, adds)
            return 0

        lax.fori_loop(0, 2, step, 0)
        copy = pltpu.make_async_copy(result.at[DOWN], out, sem)
        copy.start()
        return copy

    loads[0].wait()
    loads[1].wait()
    normalize(tok, 0, True)
    loads[2].wait()
    loads[3].wait()
    forward(0)
    loads[4].wait()
    loads[5].wait()
    backward(0)

    send_tok.wait_recv()
    normalize(normed, rows, False)
    forward(rows)
    return_out()
    send_cot.wait_recv()
    backward(rows)

    a1_step(GATE)
    bx_step(0)
    a1_step(UP)
    bx_step(1)
    bx_step(2)
    bx_step(3)
    a2_direct(GATE)
    a2_direct(UP)
    return_grad()
    a2_merged(GATE)
    b_opposite()
    a2_merged(UP)

    @pl.when(core == 1)
    def _():
        finish_rows()

    b_direct()
    b_merged()
    a_cross(GATE)
    a_cross(UP)
    stores = [b_last(down_grad, store_sem.at[2])]
    stores.append(a_last(GATE, gate_grad, store_sem.at[3]))
    stores.append(a_last(UP, up_grad, store_sem.at[4]))

    @pl.when(core == 0)
    def _():
        finish_rows()

    for copy in stores:
        copy.wait()
    store_out.wait()
    store_grad.wait()
    for copy in (send_tok, send_cot, send_out, send_grad):
        copy.wait_send()

    def drain(i, _):
        m, way = i // 2, lax.rem(i, 2)
        copy_a1(m, way).wait_send()
        for merged in range(2):
            copy_a2(m, way, merged).wait_send()
        copy_bx(i).wait_send()
        return 0

    lax.fori_loop(0, 4, drain, 0)
    for i in range(2):
        copy_ax(i).wait_send()
        copy_bz1(i).wait_send()
        copy_bz2(i, 0).wait_send()
        copy_bz2(i, 1).wait_send()


def body(sections, tokens, norm_gain, gate_weight, up_weight, down_weight, cotangent):
    rows, depth = tokens.shape
    ff = down_weight.shape[0]
    half = ff // 2
    piece = depth // 8
    anywhere = pl.BlockSpec(memory_space=pl.ANY)
    dma = pltpu.SemaphoreType.DMA

    def vmem(*shape, dtype=BF16):
        return pltpu.VMEM(shape, dtype)

    flops = 2 * 18 * rows * depth * ff
    return pl.pallas_call(
        functools.partial(kernel, sections),
        out_shape=(
            jax.ShapeDtypeStruct((rows, depth), BF16),
            jax.ShapeDtypeStruct((rows, depth), BF16),
            jax.ShapeDtypeStruct((piece, ff), F32),
            jax.ShapeDtypeStruct((piece, ff), F32),
            jax.ShapeDtypeStruct((ff, piece), F32),
        ),
        in_specs=[anywhere] * 6,
        out_specs=(anywhere,) * 5,
        scratch_shapes=[
            vmem(1, depth, dtype=F32),
            vmem(2, depth, ff),
            vmem(ff, depth),
            vmem(rows, depth),
            vmem(2 * rows, depth),
            vmem(2 * rows, depth),
            vmem(rows, 128, dtype=F32),
            vmem(rows, ff, dtype=F32),
            vmem(rows, ff, dtype=F32),
            vmem(3, 2 * rows, ff),
            vmem(3, ff, 2 * rows),
            vmem(rows, depth, dtype=F32),
            vmem(rows, depth),
            vmem(rows, depth),
            vmem(rows, depth),
            vmem(rows, depth),
            vmem(2, 2, ff, piece),
            vmem(2, 2, ff, piece),
            vmem(2, 2, ff, piece),
            vmem(2, 2, 2, ff, piece),
            vmem(2, ff, piece),
            vmem(4, ff, piece),
            vmem(4, ff, piece),
            vmem(2, half, piece),
            vmem(2, 2, half, piece),
            vmem(3, ff, piece, dtype=F32),
            dma((6,)),
            dma((5,)),
            dma((2, 2)),
            dma((2, 2)),
            dma((2, 2, 2)),
            dma((2, 2, 2, 2)),
            dma((2, 2)),
            dma((4, 2)),
            dma((2, 2)),
            dma((2, 2, 2)),
        ],
        compiler_params=pltpu.CompilerParams(
            collective_id=0, has_side_effects=True, vmem_limit_bytes=63 * 2**20
        ),
        cost_estimate=pl.CostEstimate(
            flops=flops, bytes_accessed=23 * 2**20, transcendentals=4 * rows * ff
        ),
    )(tokens, norm_gain.reshape(1, depth), gate_weight, up_weight, down_weight, cotangent)


def solution(mesh):
    in_specs = (
        P(("section", "dp"), None),
        P(),
        P(None, "section"),
        P(None, "section"),
        P("section", None),
        P(("section", "dp"), None),
    )
    out_specs = (
        P(("section", "dp"), None),
        P(("section", "dp"), None),
        P("dp", "section"),
        P("dp", "section"),
        P("section", "dp"),
    )
    return jax.shard_map(
        functools.partial(body, mesh.shape["section"]),
        mesh=mesh,
        in_specs=in_specs,
        out_specs=out_specs,
        check_vma=False,
    )
```

```python
import functools
import math

import jax
import jax.numpy as jnp
from jax import lax
from jax.experimental import pallas as pl
from jax.experimental.pallas import tpu as pltpu
from jax.sharding import PartitionSpec as P

ROUNDS = 2
GATE, UP, DOWN = 0, 1, 2
MESH = pl.DeviceIdType.MESH
F32 = jnp.float32
BF16 = jnp.bfloat16


def dot_nt(a, b):
    return lax.dot_general(a, b, (((1,), (1,)), ((), ())), preferred_element_type=F32)


def kernel(
    sections,
    tokens,
    gain_hbm,
    gate_hbm,
    up_hbm,
    down_hbm,
    cotangent,
    layer_out,
    input_grad,
    gate_grad,
    up_grad,
    down_grad,
    gain,
    weight_in,
    weight_down,
    tok,
    normed,
    cot,
    inverse,
    gate_act,
    up_act,
    acts,
    acts_t,
    scaled,
    back_out,
    back_grad,
    ret_out,
    ret_grad,
    a1_out,
    a1_in,
    a2_out,
    a2_in,
    ax_in,
    far_normed,
    far_acts,
    bo_out,
    bd_out,
    b1_in,
    b2_in,
    result,
    load_sem,
    store_sem,
    tok_sem,
    back_sem,
    a1_sem,
    a2_sem,
    ax_sem,
    near_sem,
    rest_sem,
    pass_sem,
    far_sem,
    b1_sem,
    b2_sem,
):
    rows, depth = tok.shape
    ff = weight_down.shape[0]
    half = ff // 2
    piece = depth // 8
    factor = 1.0 / math.sqrt(ROUNDS * 8 * rows)
    own, met = pl.ds(0, rows), pl.ds(rows, rows)

    s = lax.axis_index("section")
    j = lax.axis_index("dp")
    core = lax.rem(s, 2)
    z, xl = j // 2, lax.rem(j, 2)
    mirrored = j + 1 - 2 * xl
    before, after = lax.rem(s + sections - 1, sections), lax.rem(s + 1, sections)
    j_before = jnp.where(lax.rem(s, 8) == 0, mirrored, j)
    j_after = jnp.where(lax.rem(after, 8) == 0, mirrored, j)
    to_before, to_after = (before, j_before), (after, j_after)
    partner = (s, mirrored)

    def plane(by):
        return lax.rem(z + by, 4)

    def neighbour(way):
        return (s, plane(1 + 2 * way) * 2 + xl)

    def remote(src, dst, sems, device):
        return pltpu.make_async_remote_copy(
            src_ref=src,
            dst_ref=dst,
            send_sem=sems.at[0],
            recv_sem=sems.at[1],
            device_id=device,
            device_id_type=MESH,
        )

    loads = [
        pltpu.make_async_copy(src, dst, load_sem.at[i])
        for i, (src, dst) in enumerate(
            (
                (tokens, tok),
                (gain_hbm, gain),
                (gate_hbm, weight_in.at[GATE]),
                (up_hbm, weight_in.at[UP]),
                (cotangent, cot.at[pl.ds(0, rows)]),
                (down_hbm, weight_down),
            )
        )
    ]
    for load in loads:
        load.start()

    barrier = pltpu.get_barrier_semaphore()
    for device in (to_before, to_after, partner, neighbour(0), neighbour(1)):
        pl.semaphore_signal(barrier, inc=1, device_id=device, device_id_type=MESH)
    pl.semaphore_wait(barrier, 5)

    send_tok = remote(tokens, normed.at[pl.ds(rows, rows)], tok_sem.at[0], to_before)
    send_cot = remote(cotangent, cot.at[pl.ds(rows, rows)], tok_sem.at[1], to_before)
    send_out = remote(back_out, ret_out, back_sem.at[0], to_after)
    send_grad = remote(back_grad, ret_grad, back_sem.at[1], to_after)
    send_tok.start()
    send_cot.start()

    def normalize(src, first, keep):
        def step(i, _):
            at = pl.ds(pl.multiple_of(i * 16, 16), 16)
            to = pl.ds(pl.multiple_of(first + i * 16, 16), 16)
            values = (src[at] if keep else src[to]).astype(F32)
            inv = lax.rsqrt(jnp.sum(values * values, axis=1, keepdims=True) / depth + 1e-05)
            if keep:
                inverse[at] = jnp.broadcast_to(inv, (16, 128))
            normed[to] = (values * inv * gain[...]).astype(BF16)
            return 0

        lax.fori_loop(0, rows // 16, step, 0)

    def forward(first):
        here = pl.ds(first, rows)

        def step(h, _):
            cols = pl.ds(pl.multiple_of(h * half, half), half)
            g = jnp.dot(normed[here], weight_in[GATE, :, cols], preferred_element_type=F32)
            u = jnp.dot(normed[here], weight_in[UP, :, cols], preferred_element_type=F32)
            gate_act[here, cols] = g
            up_act[here, cols] = u
            hidden = g * jax.nn.sigmoid(g) * u
            acts[DOWN, here, cols] = hidden.astype(BF16)
            acts_t[DOWN, cols, here] = hidden.T.astype(BF16)
            return 0

        lax.fori_loop(0, 2, step, 0)

    def backward(first):
        here = pl.ds(first, rows)

        def step(h, _):
            cols = pl.ds(pl.multiple_of(h * half, half), half)
            grad_hidden = dot_nt(cot[here], weight_down[cols])
            g, u = gate_act[here, cols], up_act[here, cols]
            sig = jax.nn.sigmoid(g)
            grad_gate = grad_hidden * u * sig * (1.0 + g * (1.0 - sig))
            grad_up = grad_hidden * (g * sig)
            acts[GATE, here, cols] = grad_gate.astype(BF16)
            acts[UP, here, cols] = grad_up.astype(BF16)
            acts_t[GATE, cols, here] = grad_gate.T.astype(BF16)
            acts_t[UP, cols, here] = grad_up.T.astype(BF16)
            return 0

        lax.fori_loop(0, 2, step, 0)

    def chunk(c):
        return pl.ds(pl.multiple_of(c * piece, piece), piece)

    def out_chunk(first, c):
        return jnp.dot(
            acts[DOWN, pl.ds(first, rows)], weight_down[:, chunk(c)], preferred_element_type=F32
        )

    def grad_chunk(first, c):
        here = pl.ds(first, rows)
        return dot_nt(acts[GATE, here], weight_in[GATE, chunk(c)]) + dot_nt(
            acts[UP, here], weight_in[UP, chunk(c)]
        )

    def return_out():
        def step(c, _):
            back_out[:, chunk(c)] = out_chunk(rows, c).astype(BF16)
            return 0

        lax.fori_loop(0, 8, step, 0)
        send_out.start()

    def return_grad():
        def step(c, _):
            back_grad[:, chunk(c)] = grad_chunk(rows, c).astype(BF16)
            return 0

        lax.fori_loop(0, 8, step, 0)
        send_grad.start()

    store_out = pltpu.make_async_copy(ret_out, layer_out, store_sem.at[0])
    store_grad = pltpu.make_async_copy(ret_grad, input_grad, store_sem.at[1])

    def finish_out():
        send_out.wait_recv()

        def step(c, _):
            at = chunk(c)
            total = tok[:, at].astype(F32) + out_chunk(0, c) + ret_out[:, at].astype(F32)
            ret_out[:, at] = total.astype(BF16)
            return 0

        lax.fori_loop(0, 8, step, 0)
        store_out.start()

    def own_grad():
        def step(c, _):
            scaled[:, chunk(c)] = grad_chunk(0, c)
            return 0

        lax.fori_loop(0, 8, step, 0)

    def finish_grad():
        send_grad.wait_recv()

        def grad_step(c, mixed):
            at = chunk(c)
            g = (scaled[:, at] + ret_grad[:, at].astype(F32)) * gain[:, at]
            scaled[:, at] = g
            return mixed + jnp.sum(g * tok[:, at].astype(F32), axis=1, keepdims=True)

        mixed = lax.fori_loop(0, 8, grad_step, jnp.zeros((rows, 1), F32))
        inv = inverse[:, :1]
        weight = inv * inv * inv * (mixed / depth)

        def last_step(c, _):
            at = chunk(c)
            total = cot[own, at].astype(F32) + inv * scaled[:, at]
            total = total - tok[:, at].astype(F32) * weight
            ret_grad[:, at] = total.astype(BF16)
            return 0

        lax.fori_loop(0, 8, last_step, 0)
        store_grad.start()

    whole = pl.ds(0, ff)

    def half_rows(h):
        return pl.ds(pl.multiple_of(h * half, half), half)

    def into(ref):
        def put(at, acc):
            ref[:, at] = acc.astype(BF16)

        return put

    def down_tile(to_plane, to_x, put, adds):
        first = (to_plane * 2 + to_x) * piece
        for c in range(2):
            at = pl.ds(c * (piece // 2), piece // 2)
            cols = pl.ds(pl.multiple_of(first + c * (piece // 2), piece // 2), piece // 2)
            acc = jnp.dot(acts_t[DOWN], cot[:, cols], preferred_element_type=F32)
            for ref in adds:
                acc = acc + ref[:, at].astype(F32)
            put(at, acc)

    def in_tile(m, to_plane, part, put, adds):
        cols = pl.ds(pl.multiple_of((to_plane * 2 + xl) * piece, piece), piece)
        acc = jnp.dot(acts_t[m, part], normed[:, cols], preferred_element_type=F32)
        acc = acc + jnp.dot(far_acts[m, part], far_normed[to_plane], preferred_element_type=F32)
        for ref in adds:
            acc = acc + ref[...].astype(F32)
        put(pl.ds(0, piece), acc)

    def two(step):
        def run(i, _):
            step(i)
            return 0

        lax.fori_loop(0, 2, run, 0)

    def copy_a1(way):
        return remote(a1_out.at[way], a1_in.at[way], a1_sem.at[way], neighbour(way))

    def copy_a2(way, merged):
        src = a1_in.at[way] if merged else a2_out.at[way]
        return remote(src, a2_in.at[way, merged], a2_sem.at[way, merged], neighbour(way))

    copy_ax = remote(a2_in.at[0, xl], ax_in, ax_sem, partner)

    def a_opposite(way):
        down_tile(plane(2), way, into(a1_out.at[way]), ())
        copy_a1(way).start()

    def a_direct(way):
        down_tile(plane(1 + 2 * way), 1 - way, into(a2_out.at[way]), ())
        copy_a2(way, 0).start()

    def a_merged(way):
        copy_a1(way).wait_recv()
        here = a1_in.at[way]
        down_tile(plane(1 + 2 * way), way, into(here), (here,))
        copy_a2(way, 1).start()

    def a_cross():
        for way in range(2):
            for merged in range(2):
                copy_a2(way, merged).wait_recv()
        here = a2_in.at[0, xl]
        down_tile(z, 1 - xl, into(here), (here, a2_in.at[1, 1 - xl]))
        copy_ax.start()

    def store(m, out):
        copy = pltpu.make_async_copy(result.at[m], out, store_sem.at[2 + m])
        copy.start()
        return copy

    def a_last():
        copy_ax.wait_recv()

        def put(at, acc):
            result[DOWN, :, at] = (acc * factor).astype(BF16)

        down_tile(z, xl, put, (a2_in.at[0, 1 - xl], a2_in.at[1, xl], ax_in))
        return store(DOWN, down_grad)

    def far_columns(zz):
        return pl.ds(pl.multiple_of((zz * 2 + 1 - xl) * piece, piece), piece)

    def copy_near(zz):
        return remote(
            normed.at[own, far_columns(zz)], far_normed.at[zz, own], near_sem.at[zz], partner
        )

    def copy_rest(zz):
        return remote(
            normed.at[met, far_columns(zz)], far_normed.at[zz, met], rest_sem.at[zz], partner
        )

    def copy_pass(zz):
        return pltpu.make_async_remote_copy(
            src_ref=far_normed.at[zz, own],
            dst_ref=far_normed.at[zz, met],
            send_sem=pass_sem.at[zz],
            recv_sem=rest_sem.at[zz, 1],
            device_id=to_before,
            device_id_type=MESH,
        )

    def copy_far(m):
        return remote(acts_t.at[m], far_acts.at[m], far_sem.at[m], partner)

    def copy_b1(m, way):
        return remote(
            bo_out.at[m, half_rows(way)], b1_in.at[m, way], b1_sem.at[m, way], neighbour(way)
        )

    def copy_b2(m, way, merged):
        src = b1_in.at[m, way] if merged else bd_out.at[m, way]
        return remote(src, b2_in.at[m, way, merged], b2_sem.at[m, way, merged], neighbour(way))

    def b_first(m):
        copy_far(m).wait_recv()

        def opposite(way):
            part = half_rows(way)
            in_tile(m, plane(2), part, into(bo_out.at[m, part]), ())
            copy_b1(m, way).start()

        def direct(way):
            in_tile(m, plane(1 + 2 * way), half_rows(1 - way), into(bd_out.at[m, way]), ())
            copy_b2(m, way, 0).start()

        two(opposite)
        two(direct)

    def b_merged(m):
        def step(way):
            copy_b1(m, way).wait_recv()
            here = b1_in.at[m, way]
            in_tile(m, plane(1 + 2 * way), half_rows(way), into(here), (here,))
            copy_b2(m, way, 1).start()

        two(step)

    def b_last(m, out):
        for way in range(2):
            for merged in range(2):
                copy_b2(m, way, merged).wait_recv()

        def step(h):
            part = half_rows(h)

            def put(at, acc):
                result[m, part, at] = (acc * factor).astype(BF16)

            in_tile(m, z, part, put, (b2_in.at[m, 0, 1 - h], b2_in.at[m, 1, h]))

        two(step)
        return store(m, out)

    loads[0].wait()
    loads[1].wait()
    normalize(tok, 0, True)
    for zz in range(4):
        copy_near(zz).start()
    loads[2].wait()
    loads[3].wait()
    forward(0)
    loads[4].wait()
    loads[5].wait()

    @pl.when(core == 1)
    def _():
        backward(0)
        own_grad()

    send_tok.wait_recv()
    normalize(normed, rows, False)

    @pl.when(core == 1)
    def _():
        for zz in range(4):
            copy_rest(zz).start()

    forward(rows)

    @pl.when(core == 1)
    def _():
        return_out()
        for zz in range(4):
            copy_near(zz).wait_recv()
            copy_pass(zz).start()

    send_cot.wait_recv()
    two(a_opposite)
    two(a_direct)

    @pl.when(core == 0)
    def _():
        backward(0)

    backward(rows)
    copy_far(GATE).start()
    copy_far(UP).start()

    @pl.when(core == 1)
    def _():
        return_grad()

    two(a_merged)

    @pl.when(core == 0)
    def _():
        return_out()
        return_grad()
        own_grad()
        for zz in range(4):
            copy_near(zz).wait_recv()

    @pl.when(core == 1)
    def _():
        finish_out()
        finish_grad()

    for zz in range(4):
        copy_rest(zz).wait_recv()
    b_first(GATE)
    b_first(UP)
    a_cross()
    b_merged(GATE)
    b_merged(UP)
    stores = [a_last()]
    stores.append(b_last(GATE, gate_grad))
    stores.append(b_last(UP, up_grad))

    @pl.when(core == 0)
    def _():
        finish_out()
        finish_grad()

    for copy in stores:
        copy.wait()
    store_out.wait()
    store_grad.wait()
    for copy in (send_tok, send_cot, send_out, send_grad, copy_ax):
        copy.wait_send()
    for zz in range(4):
        copy_near(zz).wait_send()

    @pl.when(core == 1)
    def _():
        for zz in range(4):
            copy_rest(zz).wait_send()
            copy_pass(zz).wait_send()

    for i in range(2):
        copy_a1(i).wait_send()
        copy_far(i).wait_send()
        for k in range(2):
            copy_a2(i, k).wait_send()
            copy_b1(i, k).wait_send()
            copy_b2(i, k, 0).wait_send()
            copy_b2(i, k, 1).wait_send()


def write_out(
    layer_in,
    input_in,
    gate_in,
    up_in,
    down_in,
    layer_out,
    input_grad,
    gate_grad,
    up_grad,
    down_grad,
    near,
    far,
    sems,
):
    rows = [
        pltpu.make_async_copy(src, dst, sems.at[i])
        for i, (src, dst) in enumerate(((layer_in, layer_out), (input_in, input_grad)))
    ]
    loads = [
        pltpu.make_async_copy(src, near.at[i], sems.at[2 + i])
        for i, src in enumerate((gate_in, up_in, down_in))
    ]
    stores = [
        pltpu.make_async_copy(far.at[i], dst, sems.at[5 + i])
        for i, dst in enumerate((gate_grad, up_grad, down_grad))
    ]
    for copy in loads + rows:
        copy.start()
    for m in (GATE, UP, DOWN):
        loads[m].wait()
        if m == DOWN:
            far[m] = near[m].astype(F32)
        else:
            far[m] = near[m].astype(F32).T
        stores[m].start()
    for copy in stores + rows:
        copy.wait()


def body(sections, tokens, norm_gain, gate_weight, up_weight, down_weight, cotangent):
    rows, depth = tokens.shape
    ff = down_weight.shape[0]
    half = ff // 2
    piece = depth // 8
    anywhere = pl.BlockSpec(memory_space=pl.ANY)
    dma = pltpu.SemaphoreType.DMA

    def vmem(*shape, dtype=BF16):
        return pltpu.VMEM(shape, dtype)

    flops = 2 * 18 * rows * depth * ff
    parts = pl.pallas_call(
        functools.partial(kernel, sections),
        out_shape=(
            jax.ShapeDtypeStruct((rows, depth), BF16),
            jax.ShapeDtypeStruct((rows, depth), BF16),
            jax.ShapeDtypeStruct((ff, piece), BF16),
            jax.ShapeDtypeStruct((ff, piece), BF16),
            jax.ShapeDtypeStruct((ff, piece), BF16),
        ),
        in_specs=[anywhere] * 6,
        out_specs=(anywhere,) * 5,
        scratch_shapes=[
            vmem(1, depth, dtype=F32),
            vmem(2, depth, ff),
            vmem(ff, depth),
            vmem(rows, depth),
            vmem(2 * rows, depth),
            vmem(2 * rows, depth),
            vmem(rows, 128, dtype=F32),
            vmem(2 * rows, ff, dtype=F32),
            vmem(2 * rows, ff, dtype=F32),
            vmem(3, 2 * rows, ff),
            vmem(3, ff, 2 * rows),
            vmem(rows, depth, dtype=F32),
            vmem(rows, depth),
            vmem(rows, depth),
            vmem(rows, depth),
            vmem(rows, depth),
            vmem(2, ff, piece),
            vmem(2, ff, piece),
            vmem(2, ff, piece),
            vmem(2, 2, ff, piece),
            vmem(ff, piece),
            vmem(4, 2 * rows, piece),
            vmem(2, ff, 2 * rows),
            vmem(2, ff, piece),
            vmem(2, 2, half, piece),
            vmem(2, 2, half, piece),
            vmem(2, 2, 2, half, piece),
            vmem(3, ff, piece),
            dma((6,)),
            dma((5,)),
            dma((2, 2)),
            dma((2, 2)),
            dma((2, 2)),
            dma((2, 2, 2)),
            dma((2,)),
            dma((4, 2)),
            dma((4, 2)),
            dma((4,)),
            dma((2, 2)),
            dma((2, 2, 2)),
            dma((2, 2, 2, 2)),
        ],
        compiler_params=pltpu.CompilerParams(
            collective_id=0, has_side_effects=True, vmem_limit_bytes=63 * 2**20
        ),
        cost_estimate=pl.CostEstimate(
            flops=flops, bytes_accessed=23 * 2**20, transcendentals=4 * rows * ff
        ),
    )(tokens, norm_gain.reshape(1, depth), gate_weight, up_weight, down_weight, cotangent)
    return pl.pallas_call(
        write_out,
        out_shape=(
            jax.ShapeDtypeStruct((rows, depth), BF16),
            jax.ShapeDtypeStruct((rows, depth), BF16),
            jax.ShapeDtypeStruct((piece, ff), F32),
            jax.ShapeDtypeStruct((piece, ff), F32),
            jax.ShapeDtypeStruct((ff, piece), F32),
        ),
        in_specs=[anywhere] * 5,
        out_specs=(anywhere,) * 5,
        scratch_shapes=[vmem(3, ff, piece), vmem(3, ff, piece, dtype=F32), dma((8,))],
        compiler_params=pltpu.CompilerParams(vmem_limit_bytes=32 * 2**20),
        cost_estimate=pl.CostEstimate(flops=0, bytes_accessed=13 * 2**20, transcendentals=0),
    )(*parts)


def solution(mesh):
    in_specs = (
        P(("section", "dp"), None),
        P(),
        P(None, "section"),
        P(None, "section"),
        P("section", None),
        P(("section", "dp"), None),
    )
    out_specs = (
        P(("section", "dp"), None),
        P(("section", "dp"), None),
        P("dp", "section"),
        P("dp", "section"),
        P("section", "dp"),
    )
    return jax.shard_map(
        functools.partial(body, mesh.shape["section"]),
        mesh=mesh,
        in_specs=in_specs,
        out_specs=out_specs,
        check_vma=False,
    )
```

```python
import functools
import math

import jax
import jax.numpy as jnp
from jax import lax
from jax.experimental import pallas as pl
from jax.experimental.pallas import tpu as pltpu
from jax.sharding import PartitionSpec as P

ROUNDS = 2
GATE, UP, DOWN = 0, 1, 2
MESH = pl.DeviceIdType.MESH
F32 = jnp.float32
BF16 = jnp.bfloat16


def dot_nt(a, b):
    return lax.dot_general(a, b, (((1,), (1,)), ((), ())), preferred_element_type=F32)


def kernel(
    sections,
    tokens,
    gain_hbm,
    gate_hbm,
    up_hbm,
    down_hbm,
    cotangent,
    layer_out,
    input_grad,
    gate_grad,
    up_grad,
    down_grad,
    gain,
    weight_in,
    weight_down,
    tok,
    normed,
    cot,
    inverse,
    gate_act,
    up_act,
    acts,
    acts_t,
    scaled,
    back_out,
    back_grad,
    ret_out,
    ret_grad,
    a1_out,
    a1_in,
    a2_out,
    a2_in,
    ax_in,
    far_normed,
    far_acts,
    bo_out,
    bd_out,
    held,
    b1_in,
    b2_in,
    result,
    load_sem,
    store_sem,
    tok_sem,
    back_sem,
    a1_sem,
    a2_sem,
    ax_sem,
    near_sem,
    rest_sem,
    pass_sem,
    far_sem,
    b1_sem,
    b2_sem,
):
    rows, depth = tok.shape
    ff = weight_down.shape[0]
    half = ff // 2
    piece = depth // 8
    factor = 1.0 / math.sqrt(ROUNDS * 8 * rows)
    own, met = pl.ds(0, rows), pl.ds(rows, rows)

    s = lax.axis_index("section")
    j = lax.axis_index("dp")
    core = lax.rem(s, 2)
    z, xl = j // 2, lax.rem(j, 2)
    mirrored = j + 1 - 2 * xl
    before, after = lax.rem(s + sections - 1, sections), lax.rem(s + 1, sections)
    j_before = jnp.where(lax.rem(s, 8) == 0, mirrored, j)
    j_after = jnp.where(lax.rem(after, 8) == 0, mirrored, j)
    to_before, to_after = (before, j_before), (after, j_after)
    partner = (s, mirrored)

    def plane(by):
        return lax.rem(z + by, 4)

    def neighbour(way):
        return (s, plane(1 + 2 * way) * 2 + xl)

    def remote(src, dst, sems, device):
        return pltpu.make_async_remote_copy(
            src_ref=src,
            dst_ref=dst,
            send_sem=sems.at[0],
            recv_sem=sems.at[1],
            device_id=device,
            device_id_type=MESH,
        )

    loads = [
        pltpu.make_async_copy(src, dst, load_sem.at[i])
        for i, (src, dst) in enumerate(
            (
                (tokens, tok),
                (gain_hbm, gain),
                (gate_hbm, weight_in.at[GATE]),
                (up_hbm, weight_in.at[UP]),
                (cotangent, cot.at[pl.ds(0, rows)]),
                (down_hbm, weight_down),
            )
        )
    ]
    for load in loads:
        load.start()

    barrier = pltpu.get_barrier_semaphore()
    for device in (to_before, to_after, partner, neighbour(0), neighbour(1)):
        pl.semaphore_signal(barrier, inc=1, device_id=device, device_id_type=MESH)
    pl.semaphore_wait(barrier, 5)

    part = rows // 2
    send_tok = [
        remote(
            tokens.at[pl.ds(i * part, part)],
            normed.at[pl.ds(rows + i * part, part)],
            tok_sem.at[2 + i],
            to_before,
        )
        for i in range(2)
    ]
    send_cot = [
        remote(
            cotangent.at[pl.ds(i * part, part)],
            cot.at[pl.ds(rows + i * part, part)],
            tok_sem.at[i],
            to_before,
        )
        for i in range(2)
    ]
    send_out, send_grad = (
        [
            remote(
                src.at[pl.ds(i * part, part)],
                dst.at[pl.ds(i * part, part)],
                back_sem.at[k, i],
                to_after,
            )
            for i in range(2)
        ]
        for k, (src, dst) in enumerate(((back_out, ret_out), (back_grad, ret_grad)))
    )
    for copy in (*send_tok, *send_cot):
        copy.start()

    def normalize(src, first, count, keep):
        def step(i, _):
            at = pl.ds(pl.multiple_of(i * 16, 16), 16)
            to = pl.ds(pl.multiple_of(first + i * 16, 16), 16)
            values = (src[at] if keep else src[to]).astype(F32)
            inv = lax.rsqrt(jnp.sum(values * values, axis=1, keepdims=True) / depth + 1e-05)
            if keep:
                inverse[at] = jnp.broadcast_to(inv, (16, 128))
            normed[to] = (values * inv * gain[...]).astype(BF16)
            return 0

        lax.fori_loop(0, count // 16, step, 0, unroll=2)

    def forward(first, count):
        here = pl.ds(first, count)

        def step(h, _):
            cols = pl.ds(pl.multiple_of(h * half, half), half)
            g = jnp.dot(normed[here], weight_in[GATE, :, cols], preferred_element_type=F32)
            u = jnp.dot(normed[here], weight_in[UP, :, cols], preferred_element_type=F32)
            gate_act[here, cols] = g
            up_act[here, cols] = u
            hidden = g * jax.nn.sigmoid(g) * u
            acts[DOWN, here, cols] = hidden.astype(BF16)
            acts_t[DOWN, cols, here] = hidden.T.astype(BF16)
            return 0

        lax.fori_loop(0, 2, step, 0)

    def backward(first, count):
        here = pl.ds(first, count)

        def step(h, _):
            cols = pl.ds(pl.multiple_of(h * half, half), half)
            grad_hidden = dot_nt(cot[here], weight_down[cols])
            g, u = gate_act[here, cols], up_act[here, cols]
            sig = jax.nn.sigmoid(g)
            grad_gate = grad_hidden * u * sig * (1.0 + g * (1.0 - sig))
            grad_up = grad_hidden * (g * sig)
            acts[GATE, here, cols] = grad_gate.astype(BF16)
            acts[UP, here, cols] = grad_up.astype(BF16)
            acts_t[GATE, cols, here] = grad_gate.T.astype(BF16)
            acts_t[UP, cols, here] = grad_up.T.astype(BF16)
            return 0

        lax.fori_loop(0, 2, step, 0)

    def chunk(c):
        return pl.ds(pl.multiple_of(c * piece, piece), piece)

    def out_chunk(first, count, c):
        return jnp.dot(
            acts[DOWN, pl.ds(first, count)], weight_down[:, chunk(c)], preferred_element_type=F32
        )

    def grad_chunk(first, count, c):
        here = pl.ds(first, count)
        return dot_nt(acts[GATE, here], weight_in[GATE, chunk(c)]) + dot_nt(
            acts[UP, here], weight_in[UP, chunk(c)]
        )

    def return_out(first, count):
        def step(c, _):
            back_out[pl.ds(first, count), chunk(c)] = out_chunk(rows + first, count, c).astype(BF16)
            return 0

        lax.fori_loop(0, 8, step, 0)

    def return_grad(i):
        def step(c, _):
            back_grad[pl.ds(i * part, part), chunk(c)] = grad_chunk(
                rows + i * part, part, c
            ).astype(BF16)
            return 0

        lax.fori_loop(0, 8, step, 0)
        send_grad[i].start()

    def both_grads():
        def step(c, _):
            g = grad_chunk(0, 2 * rows, c)
            scaled[:, chunk(c)] = g[:rows]
            back_grad[:, chunk(c)] = g[rows:].astype(BF16)
            return 0

        lax.fori_loop(0, 8, step, 0)
        for copy in send_grad:
            copy.start()

    store_out = pltpu.make_async_copy(ret_out, layer_out, store_sem.at[0])
    store_grad = pltpu.make_async_copy(ret_grad, input_grad, store_sem.at[1])

    def finish_out():
        for copy in send_out:
            copy.wait_recv()

        def step(c, _):
            at = chunk(c)
            total = tok[:, at].astype(F32) + out_chunk(0, rows, c) + ret_out[:, at].astype(F32)
            ret_out[:, at] = total.astype(BF16)
            return 0

        lax.fori_loop(0, 8, step, 0)
        store_out.start()

    def own_grad():
        def step(c, _):
            scaled[:, chunk(c)] = grad_chunk(0, rows, c)
            return 0

        lax.fori_loop(0, 8, step, 0)

    def finish_grad():
        for copy in send_grad:
            copy.wait_recv()

        def grad_step(c, mixed):
            at = chunk(c)
            g = (scaled[:, at] + ret_grad[:, at].astype(F32)) * gain[:, at]
            scaled[:, at] = g
            return mixed + jnp.sum(g * tok[:, at].astype(F32), axis=1, keepdims=True)

        mixed = lax.fori_loop(0, 8, grad_step, jnp.zeros((rows, 1), F32))
        inv = inverse[:, :1]
        weight = inv * inv * inv * (mixed / depth)

        def last_step(c, _):
            at = chunk(c)
            total = cot[own, at].astype(F32) + inv * scaled[:, at]
            total = total - tok[:, at].astype(F32) * weight
            ret_grad[:, at] = total.astype(BF16)
            return 0

        lax.fori_loop(0, 8, last_step, 0)
        store_grad.start()

    whole = pl.ds(0, ff)

    def half_rows(h):
        return pl.ds(pl.multiple_of(h * half, half), half)

    def into(ref):
        def put(at, acc):
            ref[:, at] = acc.astype(BF16)

        return put

    def down_tile(to_plane, to_x, put, adds):
        first = (to_plane * 2 + to_x) * piece
        for c in range(2):
            at = pl.ds(c * (piece // 2), piece // 2)
            cols = pl.ds(pl.multiple_of(first + c * (piece // 2), piece // 2), piece // 2)
            acc = jnp.dot(acts_t[DOWN], cot[:, cols], preferred_element_type=F32)
            for ref in adds:
                acc = acc + ref[:, at].astype(F32)
            put(at, acc)

    def in_tile(m, to_plane):
        cols = pl.ds(pl.multiple_of((to_plane * 2 + xl) * piece, piece), piece)
        acc = jnp.dot(acts_t[m], normed[:, cols], preferred_element_type=F32)
        return acc + jnp.dot(far_acts[m], far_normed[to_plane], preferred_element_type=F32)

    def two(step):
        def run(i, _):
            step(i)
            return 0

        lax.fori_loop(0, 2, run, 0)

    def copy_a1(way):
        return remote(a1_out.at[way], a1_in.at[way], a1_sem.at[way], neighbour(way))

    def copy_a2(way, merged):
        src = a1_in.at[way] if merged else a2_out.at[way]
        return remote(src, a2_in.at[way, merged], a2_sem.at[way, merged], neighbour(way))

    copy_ax = remote(a2_in.at[0, xl], ax_in, ax_sem, partner)

    def a_opposite(way):
        down_tile(plane(2), way, into(a1_out.at[way]), ())
        copy_a1(way).start()

    def a_direct(way):
        down_tile(plane(1 + 2 * way), 1 - way, into(a2_out.at[way]), ())
        copy_a2(way, 0).start()

    def a_merged(way):
        copy_a1(way).wait_recv()
        here = a1_in.at[way]
        down_tile(plane(1 + 2 * way), way, into(here), (here,))
        copy_a2(way, 1).start()

    def a_cross():
        for way in range(2):
            for merged in range(2):
                copy_a2(way, merged).wait_recv()
        here = a2_in.at[0, xl]
        down_tile(z, 1 - xl, into(here), (here, a2_in.at[1, 1 - xl]))
        copy_ax.start()

    def store(m, out):
        copy = pltpu.make_async_copy(result.at[m], out, store_sem.at[2 + m])
        copy.start()
        return copy

    def a_last():
        copy_ax.wait_recv()

        def put(at, acc):
            result[DOWN, :, at] = (acc * factor).astype(BF16)

        down_tile(z, xl, put, (a2_in.at[0, 1 - xl], a2_in.at[1, xl], ax_in))
        return store(DOWN, down_grad)

    def far_columns(zz):
        return pl.ds(pl.multiple_of((zz * 2 + 1 - xl) * piece, piece), piece)

    need = (2, 1, 3, 0)

    def copy_near(zz):
        return remote(
            normed.at[own, far_columns(zz)], far_normed.at[zz, own], near_sem.at[zz], partner
        )

    def start_near(k):
        copy_near(plane(need[k])).start()

    def pass_on(k):
        copy_near(plane(need[k])).wait_recv()
        copy_pass(plane(need[k])).start()

    def copy_rest(zz):
        return remote(
            normed.at[met, far_columns(zz)], far_normed.at[zz, met], rest_sem.at[zz], partner
        )

    def copy_pass(zz):
        return pltpu.make_async_remote_copy(
            src_ref=far_normed.at[zz, own],
            dst_ref=far_normed.at[zz, met],
            send_sem=pass_sem.at[zz],
            recv_sem=rest_sem.at[zz, 1],
            device_id=to_before,
            device_id_type=MESH,
        )

    def copy_far(m):
        return remote(acts_t.at[m], far_acts.at[m], far_sem.at[m], partner)

    def copy_b1(m, way):
        return remote(
            bo_out.at[m, half_rows(way)], b1_in.at[m, way], b1_sem.at[m, way], neighbour(way)
        )

    def copy_b2(m, way, merged):
        src = b1_in.at[m, way] if merged else bd_out.at[m, way]
        return remote(src, b2_in.at[m, way, merged], b2_sem.at[m, way, merged], neighbour(way))

    own_tile = (gate_act, up_act)

    def arrived(by):
        @pl.when(core == 0)
        def _():
            copy_near(plane(by)).wait_recv()

        copy_rest(plane(by)).wait_recv()

    def b_first(m):
        copy_far(m).wait_recv()
        if m == GATE:
            arrived(2)
        bo_out[m] = in_tile(m, plane(2)).astype(BF16)
        for way in range(2):
            copy_b1(m, way).start()
        for way in range(2):
            if m == GATE:
                arrived(1 + 2 * way)
            tile = in_tile(m, plane(1 + 2 * way))
            straight, later = (tile[half:], tile[:half]) if way == 0 else (tile[:half], tile[half:])
            bd_out[m, way] = straight.astype(BF16)
            copy_b2(m, way, 0).start()
            held[m, way] = later

    def b_own():
        arrived(0)
        for m in (GATE, UP):
            own_tile[m][...] = in_tile(m, z)

    def b_merged(m):
        for way in range(2):
            copy_b1(m, way).wait_recv()
            b1_in[m, way] = (held[m, way] + b1_in[m, way].astype(F32)).astype(BF16)
            copy_b2(m, way, 1).start()

    def b_last(m, out):
        for way in range(2):
            for merged in range(2):
                copy_b2(m, way, merged).wait_recv()
        for h in range(2):
            at = pl.ds(h * half, half)
            total = own_tile[m][at] + b2_in[m, 0, 1 - h].astype(F32) + b2_in[m, 1, h].astype(F32)
            result[m, at] = (total * factor).astype(BF16)
        return store(m, out)

    loads[0].wait()
    loads[1].wait()
    normalize(tok, 0, rows, True)
    start_near(0)
    start_near(1)

    @pl.when(core == 0)
    def _():
        loads[2].wait()
        loads[3].wait()
        forward(0, rows)
        for copy in send_tok:
            copy.wait_recv()
        normalize(normed, rows, rows, False)
        forward(rows, rows)
        loads[4].wait()
        loads[5].wait()
        for copy in send_cot:
            copy.wait_recv()

    @pl.when(core == 1)
    def _():
        loads[2].wait()
        loads[3].wait()
        forward(0, rows)
        loads[4].wait()
        loads[5].wait()
        backward(0, rows)
        own_grad()
        pass_on(0)
        pass_on(1)
        start_near(2)
        for i in range(2):
            send_tok[i].wait_recv()
            start_near(3) if i == 0 else pass_on(2)
            normalize(normed, rows + i * part, part, False)
            forward(rows + i * part, part)
            return_out(i * part, part)
            send_out[i].start()
        pass_on(3)
        for by in need:
            copy_rest(plane(by)).start()
        finish_out()
        finish_grad()
        send_cot[0].wait_recv()
        backward(rows, part)
        return_grad(0)
        send_cot[1].wait_recv()

    two(a_opposite)

    @pl.when(core == 0)
    def _():
        backward(0, 2 * rows)

    @pl.when(core == 1)
    def _():
        backward(rows + part, part)

    copy_far(GATE).start()
    two(a_direct)

    @pl.when(core == 0)
    def _():
        start_near(2)

    copy_far(UP).start()
    two(a_merged)

    @pl.when(core == 1)
    def _():
        return_grad(1)

    @pl.when(core == 0)
    def _():
        start_near(3)
        return_out(0, rows)
        for copy in send_out:
            copy.start()
        both_grads()

    b_first(GATE)
    b_first(UP)

    @pl.when(core == 1)
    def _():
        a_cross()
        b_own()

    b_merged(GATE)
    b_merged(UP)

    @pl.when(core == 0)
    def _():
        a_cross()
        b_own()
        finish_out()

    stores = [a_last()]
    stores.append(b_last(GATE, gate_grad))
    stores.append(b_last(UP, up_grad))

    @pl.when(core == 0)
    def _():
        finish_grad()

    for copy in stores:
        copy.wait()
    store_out.wait()
    store_grad.wait()
    for copy in (*send_tok, *send_cot, *send_out, *send_grad, copy_ax):
        copy.wait_send()

    for zz in range(4):
        copy_near(zz).wait_send()

    @pl.when(core == 1)
    def _():
        for zz in range(4):
            copy_rest(zz).wait_send()
            copy_pass(zz).wait_send()

    for i in range(2):
        copy_a1(i).wait_send()
        copy_far(i).wait_send()
        for k in range(2):
            copy_a2(i, k).wait_send()
            copy_b1(i, k).wait_send()
            copy_b2(i, k, 0).wait_send()
            copy_b2(i, k, 1).wait_send()


def write_out(
    layer_in,
    input_in,
    gate_in,
    up_in,
    down_in,
    layer_out,
    input_grad,
    gate_grad,
    up_grad,
    down_grad,
    rows,
    near,
    far,
    sems,
):
    loads = [
        pltpu.make_async_copy(src, dst, sems.at[0, i])
        for i, (src, dst) in enumerate(
            (
                (gate_in, near.at[GATE]),
                (up_in, near.at[UP]),
                (down_in, near.at[DOWN]),
                (layer_in, rows.at[0]),
                (input_in, rows.at[1]),
            )
        )
    ]
    stores = [
        pltpu.make_async_copy(src, dst, sems.at[1, i])
        for i, (src, dst) in enumerate(
            (
                (far.at[GATE], gate_grad),
                (far.at[UP], up_grad),
                (far.at[DOWN], down_grad),
                (rows.at[0], layer_out),
                (rows.at[1], input_grad),
            )
        )
    ]
    for copy in loads:
        copy.start()
    for m in (GATE, UP, DOWN):
        loads[m].wait()
        if m == DOWN:
            far[m] = near[m].astype(F32)
        else:
            far[m] = near[m].astype(F32).T
        stores[m].start()
    for i in (3, 4):
        loads[i].wait()
        stores[i].start()
    for copy in stores:
        copy.wait()


def body(sections, tokens, norm_gain, gate_weight, up_weight, down_weight, cotangent):
    rows, depth = tokens.shape
    ff = down_weight.shape[0]
    half = ff // 2
    piece = depth // 8
    anywhere = pl.BlockSpec(memory_space=pl.ANY)
    dma = pltpu.SemaphoreType.DMA

    def vmem(*shape, dtype=BF16):
        return pltpu.VMEM(shape, dtype)

    flops = 2 * 18 * rows * depth * ff
    parts = pl.pallas_call(
        functools.partial(kernel, sections),
        out_shape=(
            jax.ShapeDtypeStruct((rows, depth), BF16),
            jax.ShapeDtypeStruct((rows, depth), BF16),
            jax.ShapeDtypeStruct((ff, piece), BF16),
            jax.ShapeDtypeStruct((ff, piece), BF16),
            jax.ShapeDtypeStruct((ff, piece), BF16),
        ),
        in_specs=[anywhere] * 6,
        out_specs=(anywhere,) * 5,
        scratch_shapes=[
            vmem(1, depth, dtype=F32),
            vmem(2, depth, ff),
            vmem(ff, depth),
            vmem(rows, depth),
            vmem(2 * rows, depth),
            vmem(2 * rows, depth),
            vmem(rows, 128, dtype=F32),
            vmem(2 * rows, ff, dtype=F32),
            vmem(2 * rows, ff, dtype=F32),
            vmem(3, 2 * rows, ff),
            vmem(3, ff, 2 * rows),
            vmem(rows, depth, dtype=F32),
            vmem(rows, depth),
            vmem(rows, depth),
            vmem(rows, depth),
            vmem(rows, depth),
            vmem(2, ff, piece),
            vmem(2, ff, piece),
            vmem(2, ff, piece),
            vmem(2, 2, ff, piece),
            vmem(ff, piece),
            vmem(4, 2 * rows, piece),
            vmem(2, ff, 2 * rows),
            vmem(2, ff, piece),
            vmem(2, 2, half, piece),
            vmem(2, 2, half, piece, dtype=F32),
            vmem(2, 2, half, piece),
            vmem(2, 2, 2, half, piece),
            vmem(3, ff, piece),
            dma((6,)),
            dma((5,)),
            dma((4, 2)),
            dma((2, 2, 2)),
            dma((2, 2)),
            dma((2, 2, 2)),
            dma((2,)),
            dma((4, 2)),
            dma((4, 2)),
            dma((4,)),
            dma((2, 2)),
            dma((2, 2, 2)),
            dma((2, 2, 2, 2)),
        ],
        compiler_params=pltpu.CompilerParams(
            collective_id=0, has_side_effects=True, vmem_limit_bytes=63 * 2**20
        ),
        cost_estimate=pl.CostEstimate(
            flops=flops, bytes_accessed=23 * 2**20, transcendentals=4 * rows * ff
        ),
    )(tokens, norm_gain.reshape(1, depth), gate_weight, up_weight, down_weight, cotangent)
    return pl.pallas_call(
        write_out,
        out_shape=(
            jax.ShapeDtypeStruct((rows, depth), BF16),
            jax.ShapeDtypeStruct((rows, depth), BF16),
            jax.ShapeDtypeStruct((piece, ff), F32),
            jax.ShapeDtypeStruct((piece, ff), F32),
            jax.ShapeDtypeStruct((ff, piece), F32),
        ),
        in_specs=[anywhere] * 5,
        out_specs=(anywhere,) * 5,
        scratch_shapes=[
            vmem(2, rows, depth),
            vmem(3, ff, piece),
            vmem(3, ff, piece, dtype=F32),
            dma((2, 5)),
        ],
        compiler_params=pltpu.CompilerParams(vmem_limit_bytes=63 * 2**20),
        cost_estimate=pl.CostEstimate(flops=0, bytes_accessed=13 * 2**20, transcendentals=0),
    )(*parts)


def solution(mesh):
    in_specs = (
        P(("section", "dp"), None),
        P(),
        P(None, "section"),
        P(None, "section"),
        P("section", None),
        P(("section", "dp"), None),
    )
    out_specs = (
        P(("section", "dp"), None),
        P(("section", "dp"), None),
        P("dp", "section"),
        P("dp", "section"),
        P("section", "dp"),
    )
    return jax.shard_map(
        functools.partial(body, mesh.shape["section"]),
        mesh=mesh,
        in_specs=in_specs,
        out_specs=out_specs,
        check_vma=False,
    )
```

```python
import functools
import math

import jax
import jax.numpy as jnp
from jax import lax
from jax.experimental import pallas as pl
from jax.experimental.pallas import tpu as pltpu
from jax.sharding import PartitionSpec as P

ROUNDS = 2
GATE, UP, DOWN = 0, 1, 2
MESH = pl.DeviceIdType.MESH
F32 = jnp.float32
BF16 = jnp.bfloat16


def dot_nt(a, b):
    return lax.dot_general(a, b, (((1,), (1,)), ((), ())), preferred_element_type=F32)


def kernel(
    sections,
    tokens,
    gain_hbm,
    gate_hbm,
    up_hbm,
    down_hbm,
    cotangent,
    layer_out,
    input_grad,
    gate_grad,
    up_grad,
    down_grad,
    gain,
    weight_in,
    weight_down,
    tok,
    normed,
    cot,
    inverse,
    gate_act,
    up_act,
    grad_hidden,
    acts,
    acts_t,
    scaled,
    back_out,
    back_grad,
    ret_out,
    ret_grad,
    a1_out,
    a1_in,
    a2_out,
    a2_in,
    ax_in,
    far_normed,
    far_acts,
    bo_out,
    bd_out,
    held,
    b1_in,
    b2_in,
    result,
    load_sem,
    store_sem,
    tok_sem,
    back_sem,
    a1_sem,
    a2_sem,
    ax_sem,
    near_sem,
    rest_sem,
    pass_sem,
    far_sem,
    b1_sem,
    b2_sem,
):
    rows, depth = tok.shape
    ff = weight_down.shape[0]
    half = ff // 2
    piece = depth // 8
    factor = 1.0 / math.sqrt(ROUNDS * 8 * rows)
    own, met = pl.ds(0, rows), pl.ds(rows, rows)

    s = lax.axis_index("section")
    j = lax.axis_index("dp")
    core = lax.rem(s, 2)
    z, xl = j // 2, lax.rem(j, 2)
    mirrored = j + 1 - 2 * xl
    before, after = lax.rem(s + sections - 1, sections), lax.rem(s + 1, sections)
    j_before = jnp.where(lax.rem(s, 8) == 0, mirrored, j)
    j_after = jnp.where(lax.rem(after, 8) == 0, mirrored, j)
    to_before, to_after = (before, j_before), (after, j_after)
    partner = (s, mirrored)

    def plane(by):
        return lax.rem(z + by, 4)

    def neighbour(way):
        return (s, plane(1 + 2 * way) * 2 + xl)

    def remote(src, dst, sems, device):
        return pltpu.make_async_remote_copy(
            src_ref=src,
            dst_ref=dst,
            send_sem=sems.at[0],
            recv_sem=sems.at[1],
            device_id=device,
            device_id_type=MESH,
        )

    loads = [
        pltpu.make_async_copy(src, dst, load_sem.at[i])
        for i, (src, dst) in enumerate(
            (
                (tokens, tok),
                (gain_hbm, gain),
                (gate_hbm, weight_in.at[GATE]),
                (up_hbm, weight_in.at[UP]),
                (cotangent, cot.at[pl.ds(0, rows)]),
                (down_hbm, weight_down),
            )
        )
    ]
    for load in loads:
        load.start()

    barrier = pltpu.get_barrier_semaphore()
    for device in (to_before, to_after, partner, neighbour(0), neighbour(1)):
        pl.semaphore_signal(barrier, inc=1, device_id=device, device_id_type=MESH)
    pl.semaphore_wait(barrier, 5)

    part = rows // 2
    send_tok = [
        remote(
            tokens.at[pl.ds(i * part, part)],
            normed.at[pl.ds(rows + i * part, part)],
            tok_sem.at[4 + i],
            to_before,
        )
        for i in range(2)
    ]
    need = (2, 1, 3, 0)

    def slab(by):
        return pl.ds(pl.multiple_of(plane(by) * 2 * piece, 2 * piece), 2 * piece)

    send_cot = [
        remote(cotangent.at[:, slab(by)], cot.at[met, slab(by)], tok_sem.at[i], to_before)
        for i, by in enumerate(need)
    ]
    send_out = [
        remote(
            back_out.at[pl.ds(i * part, part)],
            ret_out.at[pl.ds(i * part, part)],
            back_sem.at[i],
            to_after,
        )
        for i in range(2)
    ]
    send_grad = [
        remote(
            back_grad.at[:, pl.ds(i * 2 * piece, 2 * piece)],
            ret_grad.at[:, pl.ds(i * 2 * piece, 2 * piece)],
            back_sem.at[2 + i],
            to_after,
        )
        for i in range(4)
    ]
    for copy in (*send_tok, *send_cot):
        copy.start()

    def normalize(src, first, count, keep):
        def step(i, _):
            at = pl.ds(pl.multiple_of(i * 16, 16), 16)
            to = pl.ds(pl.multiple_of(first + i * 16, 16), 16)
            values = (src[at] if keep else src[to]).astype(F32)
            inv = lax.rsqrt(jnp.sum(values * values, axis=1, keepdims=True) / depth + 1e-05)
            if keep:
                inverse[at] = jnp.broadcast_to(inv, (16, 128))
            normed[to] = (values * inv * gain[...]).astype(BF16)
            return 0

        lax.fori_loop(0, count // 16, step, 0, unroll=2)

    def forward(first, count):
        here = pl.ds(first, count)

        def step(h, _):
            cols = pl.ds(pl.multiple_of(h * half, half), half)
            g = jnp.dot(normed[here], weight_in[GATE, :, cols], preferred_element_type=F32)
            u = jnp.dot(normed[here], weight_in[UP, :, cols], preferred_element_type=F32)
            gate_act[here, cols] = g
            up_act[here, cols] = u
            hidden = g * jax.nn.sigmoid(g) * u
            acts[DOWN, here, cols] = hidden.astype(BF16)
            acts_t[DOWN, cols, here] = hidden.T.astype(BF16)
            return 0

        lax.fori_loop(0, 2, step, 0)

    def backward_part(here, cols, grad_hidden):
        g, u = gate_act[here, cols], up_act[here, cols]
        sig = jax.nn.sigmoid(g)
        grad_gate = grad_hidden * u * sig * (1.0 + g * (1.0 - sig))
        grad_up = grad_hidden * (g * sig)
        acts[GATE, here, cols] = grad_gate.astype(BF16)
        acts[UP, here, cols] = grad_up.astype(BF16)
        acts_t[GATE, cols, here] = grad_gate.T.astype(BF16)
        acts_t[UP, cols, here] = grad_up.T.astype(BF16)

    def backward(first, count):
        here = pl.ds(first, count)

        def step(h, _):
            cols = pl.ds(pl.multiple_of(h * half, half), half)
            backward_part(here, cols, dot_nt(cot[here], weight_down[cols]))
            return 0

        lax.fori_loop(0, 2, step, 0)

    def met_slab(by):
        def step(h, _):
            cols = pl.ds(pl.multiple_of(h * half, half), half)
            term = dot_nt(cot[met, slab(by)], weight_down[cols, slab(by)])
            grad_hidden[:, cols] = term if by == need[0] else grad_hidden[:, cols] + term
            return 0

        lax.fori_loop(0, 2, step, 0)

    def backward_met():
        def step(h, _):
            cols = pl.ds(pl.multiple_of(h * half, half), half)
            backward_part(met, cols, grad_hidden[:, cols])
            return 0

        lax.fori_loop(0, 2, step, 0)

    def chunk(c):
        return pl.ds(pl.multiple_of(c * piece, piece), piece)

    def out_chunk(first, count, c):
        return jnp.dot(
            acts[DOWN, pl.ds(first, count)], weight_down[:, chunk(c)], preferred_element_type=F32
        )

    def grad_chunk(first, count, c):
        here = pl.ds(first, count)
        return dot_nt(acts[GATE, here], weight_in[GATE, chunk(c)]) + dot_nt(
            acts[UP, here], weight_in[UP, chunk(c)]
        )

    def return_out(first, count):
        def step(c, _):
            back_out[pl.ds(first, count), chunk(c)] = out_chunk(rows + first, count, c).astype(BF16)
            return 0

        lax.fori_loop(0, 8, step, 0)

    def return_grad():
        for i in range(4):

            def step(c, _):
                back_grad[:, chunk(c)] = grad_chunk(rows, rows, c).astype(BF16)
                return 0

            lax.fori_loop(2 * i, 2 * i + 2, step, 0)
            send_grad[i].start()

    def both_grads():
        def step(c, _):
            g = grad_chunk(0, 2 * rows, c)
            scaled[:, chunk(c)] = g[:rows]
            back_grad[:, chunk(c)] = g[rows:].astype(BF16)
            return 0

        lax.fori_loop(0, 8, step, 0)
        for copy in send_grad:
            copy.start()

    store_out = pltpu.make_async_copy(ret_out, layer_out, store_sem.at[0])
    store_grad = pltpu.make_async_copy(ret_grad, input_grad, store_sem.at[1])

    def finish_out():
        for copy in send_out:
            copy.wait_recv()

        def step(c, _):
            at = chunk(c)
            total = tok[:, at].astype(F32) + out_chunk(0, rows, c) + ret_out[:, at].astype(F32)
            ret_out[:, at] = total.astype(BF16)
            return 0

        lax.fori_loop(0, 8, step, 0)
        store_out.start()

    def own_grad():
        def step(c, _):
            scaled[:, chunk(c)] = grad_chunk(0, rows, c)
            return 0

        lax.fori_loop(0, 8, step, 0)

    def finish_grad():
        for copy in send_grad:
            copy.wait_recv()

        def grad_step(c, mixed):
            at = chunk(c)
            g = (scaled[:, at] + ret_grad[:, at].astype(F32)) * gain[:, at]
            scaled[:, at] = g
            return mixed + jnp.sum(g * tok[:, at].astype(F32), axis=1, keepdims=True)

        mixed = lax.fori_loop(0, 8, grad_step, jnp.zeros((rows, 1), F32))
        inv = inverse[:, :1]
        weight = inv * inv * inv * (mixed / depth)

        def last_step(c, _):
            at = chunk(c)
            total = cot[own, at].astype(F32) + inv * scaled[:, at]
            total = total - tok[:, at].astype(F32) * weight
            ret_grad[:, at] = total.astype(BF16)
            return 0

        lax.fori_loop(0, 8, last_step, 0)
        store_grad.start()

    whole = pl.ds(0, ff)

    def half_rows(h):
        return pl.ds(pl.multiple_of(h * half, half), half)

    def into(ref):
        def put(at, acc):
            ref[:, at] = acc.astype(BF16)

        return put

    def down_tile(to_plane, to_x, put, adds):
        first = (to_plane * 2 + to_x) * piece
        for c in range(2):
            at = pl.ds(c * (piece // 2), piece // 2)
            cols = pl.ds(pl.multiple_of(first + c * (piece // 2), piece // 2), piece // 2)
            acc = jnp.dot(acts_t[DOWN], cot[:, cols], preferred_element_type=F32)
            for ref in adds:
                acc = acc + ref[:, at].astype(F32)
            put(at, acc)

    def in_tile(m, to_plane):
        cols = pl.ds(pl.multiple_of((to_plane * 2 + xl) * piece, piece), piece)
        acc = jnp.dot(acts_t[m], normed[:, cols], preferred_element_type=F32)
        return acc + jnp.dot(far_acts[m], far_normed[to_plane], preferred_element_type=F32)

    def two(step):
        def run(i, _):
            step(i)
            return 0

        lax.fori_loop(0, 2, run, 0)

    def copy_a1(way):
        return remote(a1_out.at[way], a1_in.at[way], a1_sem.at[way], neighbour(way))

    def copy_a2(way, merged):
        src = a1_in.at[way] if merged else a2_out.at[way]
        return remote(src, a2_in.at[way, merged], a2_sem.at[way, merged], neighbour(way))

    copy_ax = remote(a2_in.at[0, xl], ax_in, ax_sem, partner)

    def a_opposite(way):
        down_tile(plane(2), way, into(a1_out.at[way]), ())
        copy_a1(way).start()

    def a_direct(way):
        down_tile(plane(1 + 2 * way), 1 - way, into(a2_out.at[way]), ())
        copy_a2(way, 0).start()

    def a_merged(way):
        copy_a1(way).wait_recv()
        here = a1_in.at[way]
        down_tile(plane(1 + 2 * way), way, into(here), (here,))
        copy_a2(way, 1).start()

    def a_cross():
        for way in range(2):
            for merged in range(2):
                copy_a2(way, merged).wait_recv()
        here = a2_in.at[0, xl]
        down_tile(z, 1 - xl, into(here), (here, a2_in.at[1, 1 - xl]))
        copy_ax.start()

    def store(m, out):
        copy = pltpu.make_async_copy(result.at[m], out, store_sem.at[2 + m])
        copy.start()
        return copy

    def a_last():
        copy_ax.wait_recv()

        def put(at, acc):
            result[DOWN, :, at] = (acc * factor).astype(BF16)

        down_tile(z, xl, put, (a2_in.at[0, 1 - xl], a2_in.at[1, xl], ax_in))
        return store(DOWN, down_grad)

    def far_columns(zz):
        return pl.ds(pl.multiple_of((zz * 2 + 1 - xl) * piece, piece), piece)

    def copy_near(zz):
        return remote(
            normed.at[own, far_columns(zz)], far_normed.at[zz, own], near_sem.at[zz], partner
        )

    def start_near(k):
        copy_near(plane(need[k])).start()

    def pass_on(k):
        copy_near(plane(need[k])).wait_recv()
        copy_pass(plane(need[k])).start()

    def copy_rest(zz):
        return remote(
            normed.at[met, far_columns(zz)], far_normed.at[zz, met], rest_sem.at[zz], partner
        )

    def copy_pass(zz):
        return pltpu.make_async_remote_copy(
            src_ref=far_normed.at[zz, own],
            dst_ref=far_normed.at[zz, met],
            send_sem=pass_sem.at[zz],
            recv_sem=rest_sem.at[zz, 1],
            device_id=to_before,
            device_id_type=MESH,
        )

    def copy_far(m):
        return remote(acts_t.at[m], far_acts.at[m], far_sem.at[m], partner)

    def copy_b1(m, way):
        return remote(
            bo_out.at[m, half_rows(way)], b1_in.at[m, way], b1_sem.at[m, way], neighbour(way)
        )

    def copy_b2(m, way, merged):
        src = b1_in.at[m, way] if merged else bd_out.at[m, way]
        return remote(src, b2_in.at[m, way, merged], b2_sem.at[m, way, merged], neighbour(way))

    own_tile = (gate_act, up_act)

    def arrived(by):
        @pl.when(core == 0)
        def _():
            copy_near(plane(by)).wait_recv()

        copy_rest(plane(by)).wait_recv()

    def b_first(m):
        copy_far(m).wait_recv()
        if m == GATE:
            arrived(2)
        bo_out[m] = in_tile(m, plane(2)).astype(BF16)
        for way in range(2):
            copy_b1(m, way).start()
        for way in range(2):
            if m == GATE:
                arrived(1 + 2 * way)
            tile = in_tile(m, plane(1 + 2 * way))
            straight, later = (tile[half:], tile[:half]) if way == 0 else (tile[:half], tile[half:])
            bd_out[m, way] = straight.astype(BF16)
            copy_b2(m, way, 0).start()
            held[m, way] = later

    def b_own():
        arrived(0)
        for m in (GATE, UP):
            own_tile[m][...] = in_tile(m, z)

    def b_merged(m):
        for way in range(2):
            copy_b1(m, way).wait_recv()
            b1_in[m, way] = (held[m, way] + b1_in[m, way].astype(F32)).astype(BF16)
            copy_b2(m, way, 1).start()

    def b_last(m, out):
        for way in range(2):
            for merged in range(2):
                copy_b2(m, way, merged).wait_recv()
        for h in range(2):
            at = pl.ds(h * half, half)
            total = own_tile[m][at] + b2_in[m, 0, 1 - h].astype(F32) + b2_in[m, 1, h].astype(F32)
            result[m, at] = (total * factor).astype(BF16)
        return store(m, out)

    loads[0].wait()
    loads[1].wait()
    normalize(tok, 0, rows, True)
    start_near(0)
    start_near(1)

    @pl.when(core == 0)
    def _():
        loads[2].wait()
        loads[3].wait()
        forward(0, rows)
        for copy in send_tok:
            copy.wait_recv()
        normalize(normed, rows, rows, False)
        forward(rows, rows)
        loads[4].wait()
        loads[5].wait()
        for copy in send_cot:
            copy.wait_recv()
        two(a_opposite)
        backward(0, 2 * rows)
        copy_far(GATE).start()
        two(a_direct)
        start_near(2)
        copy_far(UP).start()
        two(a_merged)
        start_near(3)
        return_out(0, rows)
        for copy in send_out:
            copy.start()
        both_grads()

    @pl.when(core == 1)
    def _():
        loads[2].wait()
        loads[3].wait()
        forward(0, rows)
        loads[4].wait()
        loads[5].wait()
        backward(0, rows)
        own_grad()
        pass_on(0)
        pass_on(1)
        start_near(2)
        for i in range(2):
            send_tok[i].wait_recv()
            start_near(3) if i == 0 else pass_on(2)
            normalize(normed, rows + i * part, part, False)
            forward(rows + i * part, part)
            return_out(i * part, part)
            send_out[i].start()
        pass_on(3)
        for by in need:
            copy_rest(plane(by)).start()
        send_cot[0].wait_recv()
        two(a_opposite)
        met_slab(2)
        finish_out()
        finish_grad()
        send_cot[1].wait_recv()
        a_direct(0)
        met_slab(1)
        send_cot[2].wait_recv()
        a_direct(1)
        met_slab(3)
        two(a_merged)
        send_cot[3].wait_recv()
        met_slab(0)
        backward_met()
        copy_far(GATE).start()
        copy_far(UP).start()
        return_grad()

    b_first(GATE)
    b_first(UP)

    @pl.when(core == 1)
    def _():
        a_cross()
        b_own()

    b_merged(GATE)
    b_merged(UP)

    @pl.when(core == 0)
    def _():
        a_cross()
        b_own()
        finish_out()

    stores = [a_last()]
    stores.append(b_last(GATE, gate_grad))
    stores.append(b_last(UP, up_grad))

    @pl.when(core == 0)
    def _():
        finish_grad()

    for copy in stores:
        copy.wait()
    store_out.wait()
    store_grad.wait()
    for copy in (*send_tok, *send_cot, *send_out, *send_grad, copy_ax):
        copy.wait_send()

    for zz in range(4):
        copy_near(zz).wait_send()

    @pl.when(core == 1)
    def _():
        for zz in range(4):
            copy_rest(zz).wait_send()
            copy_pass(zz).wait_send()

    for i in range(2):
        copy_a1(i).wait_send()
        copy_far(i).wait_send()
        for k in range(2):
            copy_a2(i, k).wait_send()
            copy_b1(i, k).wait_send()
            copy_b2(i, k, 0).wait_send()
            copy_b2(i, k, 1).wait_send()


def write_out(
    layer_in,
    input_in,
    gate_in,
    up_in,
    down_in,
    layer_out,
    input_grad,
    gate_grad,
    up_grad,
    down_grad,
    rows,
    near,
    far,
    sems,
):
    loads = [
        pltpu.make_async_copy(src, dst, sems.at[0, i])
        for i, (src, dst) in enumerate(
            (
                (gate_in, near.at[GATE]),
                (up_in, near.at[UP]),
                (down_in, near.at[DOWN]),
                (layer_in, rows.at[0]),
                (input_in, rows.at[1]),
            )
        )
    ]
    stores = [
        pltpu.make_async_copy(src, dst, sems.at[1, i])
        for i, (src, dst) in enumerate(
            (
                (far.at[GATE], gate_grad),
                (far.at[UP], up_grad),
                (far.at[DOWN], down_grad),
                (rows.at[0], layer_out),
                (rows.at[1], input_grad),
            )
        )
    ]
    for i in (3, 4, 0, 1, 2):
        loads[i].start()
    for i in (3, 4):
        loads[i].wait()
        stores[i].start()
    for m in (GATE, UP, DOWN):
        loads[m].wait()
        if m == DOWN:
            far[m] = near[m].astype(F32)
        else:
            far[m] = near[m].astype(F32).T
        stores[m].start()
    for copy in stores:
        copy.wait()


def body(sections, tokens, norm_gain, gate_weight, up_weight, down_weight, cotangent):
    rows, depth = tokens.shape
    ff = down_weight.shape[0]
    half = ff // 2
    piece = depth // 8
    anywhere = pl.BlockSpec(memory_space=pl.ANY)
    dma = pltpu.SemaphoreType.DMA

    def vmem(*shape, dtype=BF16):
        return pltpu.VMEM(shape, dtype)

    flops = 2 * 18 * rows * depth * ff
    parts = pl.pallas_call(
        functools.partial(kernel, sections),
        out_shape=(
            jax.ShapeDtypeStruct((rows, depth), BF16),
            jax.ShapeDtypeStruct((rows, depth), BF16),
            jax.ShapeDtypeStruct((ff, piece), BF16),
            jax.ShapeDtypeStruct((ff, piece), BF16),
            jax.ShapeDtypeStruct((ff, piece), BF16),
        ),
        in_specs=[anywhere] * 6,
        out_specs=(anywhere,) * 5,
        scratch_shapes=[
            vmem(1, depth, dtype=F32),
            vmem(2, depth, ff),
            vmem(ff, depth),
            vmem(rows, depth),
            vmem(2 * rows, depth),
            vmem(2 * rows, depth),
            vmem(rows, 128, dtype=F32),
            vmem(2 * rows, ff, dtype=F32),
            vmem(2 * rows, ff, dtype=F32),
            vmem(rows, ff, dtype=F32),
            vmem(3, 2 * rows, ff),
            vmem(3, ff, 2 * rows),
            vmem(rows, depth, dtype=F32),
            vmem(rows, depth),
            vmem(rows, depth),
            vmem(rows, depth),
            vmem(rows, depth),
            vmem(2, ff, piece),
            vmem(2, ff, piece),
            vmem(2, ff, piece),
            vmem(2, 2, ff, piece),
            vmem(ff, piece),
            vmem(4, 2 * rows, piece),
            vmem(2, ff, 2 * rows),
            vmem(2, ff, piece),
            vmem(2, 2, half, piece),
            vmem(2, 2, half, piece, dtype=F32),
            vmem(2, 2, half, piece),
            vmem(2, 2, 2, half, piece),
            vmem(3, ff, piece),
            dma((6,)),
            dma((5,)),
            dma((6, 2)),
            dma((6, 2)),
            dma((2, 2)),
            dma((2, 2, 2)),
            dma((2,)),
            dma((4, 2)),
            dma((4, 2)),
            dma((4,)),
            dma((2, 2)),
            dma((2, 2, 2)),
            dma((2, 2, 2, 2)),
        ],
        compiler_params=pltpu.CompilerParams(
            collective_id=0, has_side_effects=True, vmem_limit_bytes=63 * 2**20
        ),
        cost_estimate=pl.CostEstimate(
            flops=flops, bytes_accessed=23 * 2**20, transcendentals=4 * rows * ff
        ),
    )(tokens, norm_gain.reshape(1, depth), gate_weight, up_weight, down_weight, cotangent)
    return pl.pallas_call(
        write_out,
        out_shape=(
            jax.ShapeDtypeStruct((rows, depth), BF16),
            jax.ShapeDtypeStruct((rows, depth), BF16),
            jax.ShapeDtypeStruct((piece, ff), F32),
            jax.ShapeDtypeStruct((piece, ff), F32),
            jax.ShapeDtypeStruct((ff, piece), F32),
        ),
        in_specs=[anywhere] * 5,
        out_specs=(anywhere,) * 5,
        scratch_shapes=[
            vmem(2, rows, depth),
            vmem(3, ff, piece),
            vmem(3, ff, piece, dtype=F32),
            dma((2, 5)),
        ],
        compiler_params=pltpu.CompilerParams(vmem_limit_bytes=63 * 2**20),
        cost_estimate=pl.CostEstimate(flops=0, bytes_accessed=13 * 2**20, transcendentals=0),
    )(*parts)


def solution(mesh):
    in_specs = (
        P(("section", "dp"), None),
        P(),
        P(None, "section"),
        P(None, "section"),
        P("section", None),
        P(("section", "dp"), None),
    )
    out_specs = (
        P(("section", "dp"), None),
        P(("section", "dp"), None),
        P("dp", "section"),
        P("dp", "section"),
        P("section", "dp"),
    )
    return jax.shard_map(
        functools.partial(body, mesh.shape["section"]),
        mesh=mesh,
        in_specs=in_specs,
        out_specs=out_specs,
        check_vma=False,
    )
```

```python
import functools
import math

import jax
import jax.numpy as jnp
from jax import lax
from jax.experimental import pallas as pl
from jax.experimental.pallas import tpu as pltpu
from jax.sharding import PartitionSpec as P

ROUNDS = 2
GATE, UP, DOWN = 0, 1, 2
MESH = pl.DeviceIdType.MESH
F32 = jnp.float32
BF16 = jnp.bfloat16


def dot_nt(a, b):
    return lax.dot_general(a, b, (((1,), (1,)), ((), ())), preferred_element_type=F32)


def kernel(
    sections,
    tokens,
    gain_hbm,
    gate_hbm,
    up_hbm,
    down_hbm,
    cotangent,
    layer_out,
    input_grad,
    gate_grad,
    up_grad,
    down_grad,
    gain,
    weight_in,
    weight_down,
    tok,
    normed,
    cot,
    inverse,
    gate_act,
    up_act,
    grad_hidden,
    acts,
    acts_t,
    scaled,
    back_out,
    back_grad,
    ret_out,
    ret_grad,
    a1_out,
    a1_in,
    a2_out,
    a2_in,
    ax_in,
    far_normed,
    far_acts,
    bo_out,
    bd_out,
    held,
    b1_in,
    b2_in,
    result,
    load_sem,
    store_sem,
    tok_sem,
    back_sem,
    a1_sem,
    a2_sem,
    ax_sem,
    near_sem,
    rest_sem,
    pass_sem,
    far_sem,
    b1_sem,
    b2_sem,
):
    rows, depth = tok.shape
    ff = weight_down.shape[0]
    half = ff // 2
    piece = depth // 8
    factor = 1.0 / math.sqrt(ROUNDS * 8 * rows)
    own, met = pl.ds(0, rows), pl.ds(rows, rows)

    s = lax.axis_index("section")
    j = lax.axis_index("dp")
    core = lax.rem(s, 2)
    z, xl = j // 2, lax.rem(j, 2)
    mirrored = j + 1 - 2 * xl
    before, after = lax.rem(s + sections - 1, sections), lax.rem(s + 1, sections)
    j_before = jnp.where(lax.rem(s, 8) == 0, mirrored, j)
    j_after = jnp.where(lax.rem(after, 8) == 0, mirrored, j)
    to_before, to_after = (before, j_before), (after, j_after)
    partner = (s, mirrored)

    def plane(by):
        return lax.rem(z + by, 4)

    def neighbour(way):
        return (s, plane(1 + 2 * way) * 2 + xl)

    def remote(src, dst, sems, device):
        return pltpu.make_async_remote_copy(
            src_ref=src,
            dst_ref=dst,
            send_sem=sems.at[0],
            recv_sem=sems.at[1],
            device_id=device,
            device_id_type=MESH,
        )

    def load(i, src, dst):
        return pltpu.make_async_copy(src, dst, load_sem.at[i])

    load_rows = (load(0, tokens, tok), load(1, gain_hbm, gain))
    load_in = [
        load(2 + 2 * h + m, src.at[:, at], weight_in.at[m, :, at])
        for h, at in enumerate((pl.ds(0, half), pl.ds(half, half)))
        for m, src in enumerate((gate_hbm, up_hbm))
    ]
    load_rest = (load(6, cotangent, cot.at[own]), load(7, down_hbm, weight_down))
    for copy in (*load_rows, *load_in):
        copy.start()

    barrier = pltpu.get_barrier_semaphore()
    for device in (to_before, to_after, partner, neighbour(0), neighbour(1)):
        pl.semaphore_signal(barrier, inc=1, device_id=device, device_id_type=MESH)
    pl.semaphore_wait(barrier, 5)

    part = rows // 2
    send_tok = [
        remote(
            tokens.at[pl.ds(i * part, part)],
            normed.at[pl.ds(rows + i * part, part)],
            tok_sem.at[4 + i],
            to_before,
        )
        for i in range(2)
    ]
    need = (2, 1, 3, 0)

    def slab(by):
        return pl.ds(pl.multiple_of(plane(by) * 2 * piece, 2 * piece), 2 * piece)

    send_cot = [
        remote(cotangent.at[:, slab(by)], cot.at[met, slab(by)], tok_sem.at[i], to_before)
        for i, by in enumerate(need)
    ]
    send_out = [
        remote(
            back_out.at[pl.ds(i * part, part)],
            ret_out.at[pl.ds(i * part, part)],
            back_sem.at[i],
            to_after,
        )
        for i in range(2)
    ]
    send_grad = [
        remote(
            back_grad.at[:, pl.ds(i * 2 * piece, 2 * piece)],
            ret_grad.at[:, pl.ds(i * 2 * piece, 2 * piece)],
            back_sem.at[2 + i],
            to_after,
        )
        for i in range(4)
    ]
    for copy in (*send_tok, *send_cot):
        copy.start()

    def normalize(src, first, count, keep):
        def step(i, _):
            at = pl.ds(pl.multiple_of(i * 16, 16), 16)
            to = pl.ds(pl.multiple_of(first + i * 16, 16), 16)
            values = (src[at] if keep else src[to]).astype(F32)
            inv = lax.rsqrt(jnp.sum(values * values, axis=1, keepdims=True) / depth + 1e-05)
            if keep:
                inverse[at] = jnp.broadcast_to(inv, (16, 128))
            normed[to] = (values * inv * gain[...]).astype(BF16)
            return 0

        lax.fori_loop(0, count // 16, step, 0, unroll=2)

    def forward(first, count, fresh=False, then=None):
        here = pl.ds(first, count)

        def step(h, _):
            if fresh:
                for m in range(2):

                    @pl.when(h == 0)
                    def _():
                        load_in[m].wait()

                    @pl.when(h == 1)
                    def _():
                        load_in[2 + m].wait()

            cols = pl.ds(pl.multiple_of(h * half, half), half)
            g = jnp.dot(normed[here], weight_in[GATE, :, cols], preferred_element_type=F32)
            u = jnp.dot(normed[here], weight_in[UP, :, cols], preferred_element_type=F32)
            gate_act[here, cols] = g
            up_act[here, cols] = u
            hidden = g * jax.nn.sigmoid(g) * u
            acts[DOWN, here, cols] = hidden.astype(BF16)
            acts_t[DOWN, cols, here] = hidden.T.astype(BF16)
            if then is not None:
                then(h)
            return 0

        lax.fori_loop(0, 2, step, 0)

    def backward_part(here, cols, grad_hidden):
        g, u = gate_act[here, cols], up_act[here, cols]
        sig = jax.nn.sigmoid(g)
        grad_gate = grad_hidden * u * sig * (1.0 + g * (1.0 - sig))
        grad_up = grad_hidden * (g * sig)
        acts[GATE, here, cols] = grad_gate.astype(BF16)
        acts[UP, here, cols] = grad_up.astype(BF16)
        acts_t[GATE, cols, here] = grad_gate.T.astype(BF16)
        acts_t[UP, cols, here] = grad_up.T.astype(BF16)

    def backward(first, count):
        here = pl.ds(first, count)

        def step(h, _):
            cols = pl.ds(pl.multiple_of(h * half, half), half)
            backward_part(here, cols, dot_nt(cot[here], weight_down[cols]))
            return 0

        lax.fori_loop(0, 2, step, 0)

    def met_slab(by):
        def step(h, _):
            cols = pl.ds(pl.multiple_of(h * half, half), half)
            term = dot_nt(cot[met, slab(by)], weight_down[cols, slab(by)])
            grad_hidden[:, cols] = term if by == need[0] else grad_hidden[:, cols] + term
            return 0

        lax.fori_loop(0, 2, step, 0)

    def backward_met():
        def step(h, _):
            cols = pl.ds(pl.multiple_of(h * half, half), half)
            backward_part(met, cols, grad_hidden[:, cols])
            return 0

        lax.fori_loop(0, 2, step, 0)

    def chunk(c):
        return pl.ds(pl.multiple_of(c * piece, piece), piece)

    def out_chunk(first, count, c):
        return jnp.dot(
            acts[DOWN, pl.ds(first, count)], weight_down[:, chunk(c)], preferred_element_type=F32
        )

    def grad_chunk(first, count, c):
        here = pl.ds(first, count)
        return dot_nt(acts[GATE, here], weight_in[GATE, chunk(c)]) + dot_nt(
            acts[UP, here], weight_in[UP, chunk(c)]
        )

    def return_out(first, count):
        def step(c, _):
            back_out[pl.ds(first, count), chunk(c)] = out_chunk(rows + first, count, c).astype(BF16)
            return 0

        lax.fori_loop(0, 8, step, 0)

    def return_grad():
        for i in range(4):

            def step(c, _):
                back_grad[:, chunk(c)] = grad_chunk(rows, rows, c).astype(BF16)
                return 0

            lax.fori_loop(2 * i, 2 * i + 2, step, 0)
            send_grad[i].start()

    def both_grads():
        def step(c, _):
            g = grad_chunk(0, 2 * rows, c)
            scaled[:, chunk(c)] = g[:rows]
            back_grad[:, chunk(c)] = g[rows:].astype(BF16)
            return 0

        lax.fori_loop(0, 8, step, 0)
        for copy in send_grad:
            copy.start()

    store_out = pltpu.make_async_copy(ret_out, layer_out, store_sem.at[0])
    store_grad = pltpu.make_async_copy(ret_grad, input_grad, store_sem.at[1])

    def finish_out():
        for copy in send_out:
            copy.wait_recv()

        def step(c, _):
            at = chunk(c)
            total = tok[:, at].astype(F32) + out_chunk(0, rows, c) + ret_out[:, at].astype(F32)
            ret_out[:, at] = total.astype(BF16)
            return 0

        lax.fori_loop(0, 8, step, 0)
        store_out.start()

    def own_grad():
        def step(c, _):
            scaled[:, chunk(c)] = grad_chunk(0, rows, c)
            return 0

        lax.fori_loop(0, 8, step, 0)

    def finish_grad():
        for copy in send_grad:
            copy.wait_recv()

        def grad_step(c, mixed):
            at = chunk(c)
            g = (scaled[:, at] + ret_grad[:, at].astype(F32)) * gain[:, at]
            scaled[:, at] = g
            return mixed + jnp.sum(g * tok[:, at].astype(F32), axis=1, keepdims=True)

        mixed = lax.fori_loop(0, 8, grad_step, jnp.zeros((rows, 1), F32))
        inv = inverse[:, :1]
        weight = inv * inv * inv * (mixed / depth)

        def last_step(c, _):
            at = chunk(c)
            total = cot[own, at].astype(F32) + inv * scaled[:, at]
            total = total - tok[:, at].astype(F32) * weight
            ret_grad[:, at] = total.astype(BF16)
            return 0

        lax.fori_loop(0, 8, last_step, 0)
        store_grad.start()

    whole = pl.ds(0, ff)

    def half_rows(h):
        return pl.ds(pl.multiple_of(h * half, half), half)

    def into(ref):
        def put(at, acc):
            ref[:, at] = acc.astype(BF16)

        return put

    def down_tile(to_plane, to_x, put, adds, part=whole):
        first = (to_plane * 2 + to_x) * piece
        for c in range(2):
            at = pl.ds(c * (piece // 2), piece // 2)
            cols = pl.ds(pl.multiple_of(first + c * (piece // 2), piece // 2), piece // 2)
            acc = jnp.dot(acts_t[DOWN, part], cot[:, cols], preferred_element_type=F32)
            for ref in adds:
                acc = acc + ref[:, at].astype(F32)
            put(at, acc)

    def in_tile(m, to_plane):
        cols = pl.ds(pl.multiple_of((to_plane * 2 + xl) * piece, piece), piece)
        acc = jnp.dot(acts_t[m], normed[:, cols], preferred_element_type=F32)
        return acc + jnp.dot(far_acts[m], far_normed[to_plane], preferred_element_type=F32)

    def two(step):
        def run(i, _):
            step(i)
            return 0

        lax.fori_loop(0, 2, run, 0)

    def copy_a1(way, h):
        at = half_rows(h)
        return remote(a1_out.at[way, at], a1_in.at[way, at], a1_sem.at[way, h], neighbour(way))

    def copy_a2(way, merged):
        src = a1_in.at[way] if merged else a2_out.at[way]
        return remote(src, a2_in.at[way, merged], a2_sem.at[way, merged], neighbour(way))

    copy_ax = remote(a2_in.at[0, xl], ax_in, ax_sem, partner)

    def a_opposite(h):
        at = half_rows(h)

        def send(way):
            down_tile(plane(2), way, into(a1_out.at[way, at]), (), at)
            copy_a1(way, h).start()

        two(send)

    def a_direct(way):
        down_tile(plane(1 + 2 * way), 1 - way, into(a2_out.at[way]), ())
        copy_a2(way, 0).start()

    def a_merged(way):
        copy_a1(way, 0).wait_recv()
        copy_a1(way, 1).wait_recv()
        here = a1_in.at[way]
        down_tile(plane(1 + 2 * way), way, into(here), (here,))
        copy_a2(way, 1).start()

    def a_cross():
        for way in range(2):
            for merged in range(2):
                copy_a2(way, merged).wait_recv()
        here = a2_in.at[0, xl]
        down_tile(z, 1 - xl, into(here), (here, a2_in.at[1, 1 - xl]))
        copy_ax.start()

    def store(m, out):
        copy = pltpu.make_async_copy(result.at[m], out, store_sem.at[2 + m])
        copy.start()
        return copy

    def a_last():
        copy_ax.wait_recv()

        def put(at, acc):
            result[DOWN, :, at] = (acc * factor).astype(BF16)

        down_tile(z, xl, put, (a2_in.at[0, 1 - xl], a2_in.at[1, xl], ax_in))
        return store(DOWN, down_grad)

    def far_columns(zz):
        return pl.ds(pl.multiple_of((zz * 2 + 1 - xl) * piece, piece), piece)

    def copy_near(zz):
        return remote(
            normed.at[own, far_columns(zz)], far_normed.at[zz, own], near_sem.at[zz], partner
        )

    def start_near(k):
        copy_near(plane(need[k])).start()

    def pass_on(k):
        copy_near(plane(need[k])).wait_recv()
        copy_pass(plane(need[k])).start()

    def copy_rest(zz):
        return remote(
            normed.at[met, far_columns(zz)], far_normed.at[zz, met], rest_sem.at[zz], partner
        )

    def copy_pass(zz):
        return pltpu.make_async_remote_copy(
            src_ref=far_normed.at[zz, own],
            dst_ref=far_normed.at[zz, met],
            send_sem=pass_sem.at[zz],
            recv_sem=rest_sem.at[zz, 1],
            device_id=to_before,
            device_id_type=MESH,
        )

    def copy_far(m):
        return remote(acts_t.at[m], far_acts.at[m], far_sem.at[m], partner)

    def copy_b1(m, way):
        return remote(
            bo_out.at[m, half_rows(way)], b1_in.at[m, way], b1_sem.at[m, way], neighbour(way)
        )

    def copy_b2(m, way, merged):
        src = b1_in.at[m, way] if merged else bd_out.at[m, way]
        return remote(src, b2_in.at[m, way, merged], b2_sem.at[m, way, merged], neighbour(way))

    own_tile = (gate_act, up_act)

    def arrived(by):
        @pl.when(core == 0)
        def _():
            copy_near(plane(by)).wait_recv()

        copy_rest(plane(by)).wait_recv()

    def b_first(m):
        copy_far(m).wait_recv()
        if m == GATE:
            arrived(2)
        bo_out[m] = in_tile(m, plane(2)).astype(BF16)
        for way in range(2):
            copy_b1(m, way).start()
        for way in range(2):
            if m == GATE:
                arrived(1 + 2 * way)
            tile = in_tile(m, plane(1 + 2 * way))
            straight, later = (tile[half:], tile[:half]) if way == 0 else (tile[:half], tile[half:])
            bd_out[m, way] = straight.astype(BF16)
            copy_b2(m, way, 0).start()
            held[m, way] = later

    def b_own():
        arrived(0)
        for m in (GATE, UP):
            own_tile[m][...] = in_tile(m, z)

    def b_merged(m):
        for way in range(2):
            copy_b1(m, way).wait_recv()
            b1_in[m, way] = (held[m, way] + b1_in[m, way].astype(F32)).astype(BF16)
            copy_b2(m, way, 1).start()

    def b_last(m, out):
        for way in range(2):
            for merged in range(2):
                copy_b2(m, way, merged).wait_recv()
        for h in range(2):
            at = pl.ds(h * half, half)
            total = own_tile[m][at] + b2_in[m, 0, 1 - h].astype(F32) + b2_in[m, 1, h].astype(F32)
            result[m, at] = (total * factor).astype(BF16)
        return store(m, out)

    for copy in load_rows:
        copy.wait()
    for copy in load_rest:
        copy.start()
    normalize(tok, 0, rows, True)
    start_near(0)
    start_near(1)

    @pl.when(core == 0)
    def _():
        forward(0, rows, True)
        for copy in send_tok:
            copy.wait_recv()
        normalize(normed, rows, rows, False)
        for copy in load_rest:
            copy.wait()
        send_cot[0].wait_recv()
        forward(rows, rows, then=a_opposite)
        for copy in send_cot[1:]:
            copy.wait_recv()
        backward(0, 2 * rows)
        copy_far(GATE).start()
        two(a_direct)
        start_near(2)
        copy_far(UP).start()
        two(a_merged)
        start_near(3)
        return_out(0, rows)
        for copy in send_out:
            copy.start()
        both_grads()

    @pl.when(core == 1)
    def _():
        forward(0, rows, True)
        for copy in load_rest:
            copy.wait()
        backward(0, rows)
        own_grad()
        pass_on(0)
        pass_on(1)
        start_near(2)
        for i in range(2):
            send_tok[i].wait_recv()
            start_near(3) if i == 0 else pass_on(2)
            normalize(normed, rows + i * part, part, False)
            forward(rows + i * part, part)
            return_out(i * part, part)
            send_out[i].start()
        pass_on(3)
        for by in need:
            copy_rest(plane(by)).start()
        send_cot[0].wait_recv()
        two(a_opposite)
        met_slab(2)
        finish_out()
        finish_grad()
        send_cot[1].wait_recv()
        a_direct(0)
        met_slab(1)
        send_cot[2].wait_recv()
        a_direct(1)
        met_slab(3)
        two(a_merged)
        send_cot[3].wait_recv()
        met_slab(0)
        backward_met()
        copy_far(GATE).start()
        copy_far(UP).start()
        return_grad()

    b_first(GATE)
    b_first(UP)

    @pl.when(core == 1)
    def _():
        a_cross()
        b_own()

    b_merged(GATE)
    b_merged(UP)

    @pl.when(core == 0)
    def _():
        a_cross()
        b_own()
        finish_out()

    stores = [a_last()]
    stores.append(b_last(GATE, gate_grad))
    stores.append(b_last(UP, up_grad))

    @pl.when(core == 0)
    def _():
        finish_grad()

    for copy in stores:
        copy.wait()
    store_out.wait()
    store_grad.wait()
    for copy in (*send_tok, *send_cot, *send_out, *send_grad, copy_ax):
        copy.wait_send()

    for zz in range(4):
        copy_near(zz).wait_send()

    @pl.when(core == 1)
    def _():
        for zz in range(4):
            copy_rest(zz).wait_send()
            copy_pass(zz).wait_send()

    for i in range(2):
        copy_a1(i, 0).wait_send()
        copy_a1(i, 1).wait_send()
        copy_far(i).wait_send()
        for k in range(2):
            copy_a2(i, k).wait_send()
            copy_b1(i, k).wait_send()
            copy_b2(i, k, 0).wait_send()
            copy_b2(i, k, 1).wait_send()


def write_out(
    layer_in,
    input_in,
    gate_in,
    up_in,
    down_in,
    layer_out,
    input_grad,
    gate_grad,
    up_grad,
    down_grad,
    rows,
    near,
    far,
    sems,
):
    pieces = 4
    count = layer_in.shape[0] // pieces
    moves = []
    for k, (src, dst) in enumerate(((layer_in, layer_out), (input_in, input_grad))):
        for i in range(pieces):
            at, sem = pl.ds(i * count, count), 3 + k * pieces + i
            moves.append(
                (
                    pltpu.make_async_copy(src.at[at], rows.at[k, at], sems.at[0, sem]),
                    pltpu.make_async_copy(rows.at[k, at], dst.at[at], sems.at[1, sem]),
                )
            )
    grads = [
        (
            pltpu.make_async_copy(src, near.at[m], sems.at[0, m]),
            pltpu.make_async_copy(far.at[m], dst, sems.at[1, m]),
        )
        for m, (src, dst) in enumerate(
            ((gate_in, gate_grad), (up_in, up_grad), (down_in, down_grad))
        )
    ]
    for load, _ in grads + moves:
        load.start()
    for m, (load, store) in enumerate(grads):
        load.wait()
        if m == DOWN:
            far[m] = near[m].astype(F32)
        else:
            far[m] = near[m].astype(F32).T
        store.start()
    for load, store in moves:
        load.wait()
        store.start()
    for _, store in grads + moves:
        store.wait()


def body(sections, tokens, norm_gain, gate_weight, up_weight, down_weight, cotangent):
    rows, depth = tokens.shape
    ff = down_weight.shape[0]
    half = ff // 2
    piece = depth // 8
    anywhere = pl.BlockSpec(memory_space=pl.ANY)
    dma = pltpu.SemaphoreType.DMA

    def vmem(*shape, dtype=BF16):
        return pltpu.VMEM(shape, dtype)

    flops = 2 * 18 * rows * depth * ff
    parts = pl.pallas_call(
        functools.partial(kernel, sections),
        out_shape=(
            jax.ShapeDtypeStruct((rows, depth), BF16),
            jax.ShapeDtypeStruct((rows, depth), BF16),
            jax.ShapeDtypeStruct((ff, piece), BF16),
            jax.ShapeDtypeStruct((ff, piece), BF16),
            jax.ShapeDtypeStruct((ff, piece), BF16),
        ),
        in_specs=[anywhere] * 6,
        out_specs=(anywhere,) * 5,
        scratch_shapes=[
            vmem(1, depth, dtype=F32),
            vmem(2, depth, ff),
            vmem(ff, depth),
            vmem(rows, depth),
            vmem(2 * rows, depth),
            vmem(2 * rows, depth),
            vmem(rows, 128, dtype=F32),
            vmem(2 * rows, ff, dtype=F32),
            vmem(2 * rows, ff, dtype=F32),
            vmem(rows, ff, dtype=F32),
            vmem(3, 2 * rows, ff),
            vmem(3, ff, 2 * rows),
            vmem(rows, depth, dtype=F32),
            vmem(rows, depth),
            vmem(rows, depth),
            vmem(rows, depth),
            vmem(rows, depth),
            vmem(2, ff, piece),
            vmem(2, ff, piece),
            vmem(2, ff, piece),
            vmem(2, 2, ff, piece),
            vmem(ff, piece),
            vmem(4, 2 * rows, piece),
            vmem(2, ff, 2 * rows),
            vmem(2, ff, piece),
            vmem(2, 2, half, piece),
            vmem(2, 2, half, piece, dtype=F32),
            vmem(2, 2, half, piece),
            vmem(2, 2, 2, half, piece),
            vmem(3, ff, piece),
            dma((8,)),
            dma((5,)),
            dma((6, 2)),
            dma((6, 2)),
            dma((2, 2, 2)),
            dma((2, 2, 2)),
            dma((2,)),
            dma((4, 2)),
            dma((4, 2)),
            dma((4,)),
            dma((2, 2)),
            dma((2, 2, 2)),
            dma((2, 2, 2, 2)),
        ],
        compiler_params=pltpu.CompilerParams(
            collective_id=0, has_side_effects=True, vmem_limit_bytes=63 * 2**20
        ),
        cost_estimate=pl.CostEstimate(
            flops=flops, bytes_accessed=23 * 2**20, transcendentals=4 * rows * ff
        ),
    )(tokens, norm_gain.reshape(1, depth), gate_weight, up_weight, down_weight, cotangent)
    return pl.pallas_call(
        write_out,
        out_shape=(
            jax.ShapeDtypeStruct((rows, depth), BF16),
            jax.ShapeDtypeStruct((rows, depth), BF16),
            jax.ShapeDtypeStruct((piece, ff), F32),
            jax.ShapeDtypeStruct((piece, ff), F32),
            jax.ShapeDtypeStruct((ff, piece), F32),
        ),
        in_specs=[anywhere] * 5,
        out_specs=(anywhere,) * 5,
        scratch_shapes=[
            vmem(2, rows, depth),
            vmem(3, ff, piece),
            vmem(3, ff, piece, dtype=F32),
            dma((2, 11)),
        ],
        compiler_params=pltpu.CompilerParams(vmem_limit_bytes=63 * 2**20),
        cost_estimate=pl.CostEstimate(flops=0, bytes_accessed=13 * 2**20, transcendentals=0),
    )(*parts)


def solution(mesh):
    in_specs = (
        P(("section", "dp"), None),
        P(),
        P(None, "section"),
        P(None, "section"),
        P("section", None),
        P(("section", "dp"), None),
    )
    out_specs = (
        P(("section", "dp"), None),
        P(("section", "dp"), None),
        P("dp", "section"),
        P("dp", "section"),
        P("section", "dp"),
    )
    return jax.shard_map(
        functools.partial(body, mesh.shape["section"]),
        mesh=mesh,
        in_specs=in_specs,
        out_specs=out_specs,
        check_vma=False,
    )
```

```python
import functools
import math

import jax
import jax.numpy as jnp
from jax import lax
from jax.experimental import pallas as pl
from jax.experimental.pallas import tpu as pltpu
from jax.sharding import PartitionSpec as P

ROUNDS = 2
GATE, UP, DOWN = 0, 1, 2
MESH = pl.DeviceIdType.MESH
F32 = jnp.float32
BF16 = jnp.bfloat16


def dot_nt(a, b):
    return lax.dot_general(a, b, (((1,), (1,)), ((), ())), preferred_element_type=F32)


def kernel(
    sections,
    tokens,
    gain_hbm,
    gate_hbm,
    up_hbm,
    down_hbm,
    cotangent,
    layer_out,
    input_grad,
    gate_grad,
    up_grad,
    down_grad,
    gain,
    weight_in,
    weight_down,
    tok,
    normed,
    cot,
    inverse,
    gate_act,
    up_act,
    grad_hidden,
    acts,
    acts_t,
    scaled,
    back_out,
    back_grad,
    ret_out,
    ret_grad,
    a1_out,
    a1_in,
    a2_out,
    a2_in,
    ax_in,
    far_normed,
    far_acts,
    bo_out,
    bd_out,
    held,
    b1_in,
    b2_in,
    result,
    load_sem,
    store_sem,
    tok_sem,
    back_sem,
    a1_sem,
    a2_sem,
    ax_sem,
    near_sem,
    rest_sem,
    pass_sem,
    far_sem,
    b1_sem,
    b2_sem,
):
    rows, depth = tok.shape
    ff = weight_down.shape[0]
    half = ff // 2
    piece = depth // 8
    factor = 1.0 / math.sqrt(ROUNDS * 8 * rows)
    own, met = pl.ds(0, rows), pl.ds(rows, rows)

    s = lax.axis_index("section")
    j = lax.axis_index("dp")
    core = lax.rem(s, 2)
    z, xl = j // 2, lax.rem(j, 2)
    mirrored = j + 1 - 2 * xl
    before, after = lax.rem(s + sections - 1, sections), lax.rem(s + 1, sections)
    j_before = jnp.where(lax.rem(s, 8) == 0, mirrored, j)
    j_after = jnp.where(lax.rem(after, 8) == 0, mirrored, j)
    to_before, to_after = (before, j_before), (after, j_after)
    partner = (s, mirrored)

    def plane(by):
        return lax.rem(z + by, 4)

    def neighbour(way):
        return (s, plane(1 + 2 * way) * 2 + xl)

    def remote(src, dst, sems, device):
        return pltpu.make_async_remote_copy(
            src_ref=src,
            dst_ref=dst,
            send_sem=sems.at[0],
            recv_sem=sems.at[1],
            device_id=device,
            device_id_type=MESH,
        )

    def load(i, src, dst):
        return pltpu.make_async_copy(src, dst, load_sem.at[i])

    load_rows = (load(0, tokens, tok), load(1, gain_hbm, gain))
    load_in = [
        load(2 + 2 * h + m, src.at[:, at], weight_in.at[m, :, at])
        for h, at in enumerate((pl.ds(0, half), pl.ds(half, half)))
        for m, src in enumerate((gate_hbm, up_hbm))
    ]
    load_rest = (load(6, cotangent, cot.at[own]), load(7, down_hbm, weight_down))
    for copy in (*load_rows, *load_in):
        copy.start()

    barrier = pltpu.get_barrier_semaphore()
    for device in (to_before, to_after, partner, neighbour(0), neighbour(1)):
        pl.semaphore_signal(barrier, inc=1, device_id=device, device_id_type=MESH)
    pl.semaphore_wait(barrier, 5)

    part = rows // 2
    send_tok = [
        remote(
            tokens.at[pl.ds(i * part, part)],
            normed.at[pl.ds(rows + i * part, part)],
            tok_sem.at[4 + i],
            to_before,
        )
        for i in range(2)
    ]
    need = (2, 1, 3, 0)

    def slab(by):
        return pl.ds(pl.multiple_of(plane(by) * 2 * piece, 2 * piece), 2 * piece)

    send_cot = [
        remote(cotangent.at[:, slab(by)], cot.at[met, slab(by)], tok_sem.at[i], to_before)
        for i, by in enumerate(need)
    ]
    send_out = [
        remote(
            back_out.at[pl.ds(i * part, part)],
            ret_out.at[pl.ds(i * part, part)],
            back_sem.at[i],
            to_after,
        )
        for i in range(2)
    ]
    send_grad = [
        remote(
            back_grad.at[:, pl.ds(i * 2 * piece, 2 * piece)],
            ret_grad.at[:, pl.ds(i * 2 * piece, 2 * piece)],
            back_sem.at[2 + i],
            to_after,
        )
        for i in range(4)
    ]
    for copy in (*send_tok, *send_cot):
        copy.start()

    def normalize(src, first, count, keep):
        def step(i, _):
            at = pl.ds(pl.multiple_of(i * 16, 16), 16)
            to = pl.ds(pl.multiple_of(first + i * 16, 16), 16)
            values = (src[at] if keep else src[to]).astype(F32)
            inv = lax.rsqrt(jnp.sum(values * values, axis=1, keepdims=True) / depth + 1e-05)
            if keep:
                inverse[at] = jnp.broadcast_to(inv, (16, 128))
            normed[to] = (values * inv * gain[...]).astype(BF16)
            return 0

        lax.fori_loop(0, count // 16, step, 0, unroll=4)

    def forward(first, count, fresh=False, then=None):
        here = pl.ds(first, count)

        def step(h, _):
            if fresh:
                for m in range(2):

                    @pl.when(h == 0)
                    def _():
                        load_in[m].wait()

                    @pl.when(h == 1)
                    def _():
                        load_in[2 + m].wait()

            cols = pl.ds(pl.multiple_of(h * half, half), half)
            g = jnp.dot(normed[here], weight_in[GATE, :, cols], preferred_element_type=F32)
            u = jnp.dot(normed[here], weight_in[UP, :, cols], preferred_element_type=F32)
            gate_act[here, cols] = g
            up_act[here, cols] = u
            hidden = g * jax.nn.sigmoid(g) * u
            acts[DOWN, here, cols] = hidden.astype(BF16)
            acts_t[DOWN, cols, here] = hidden.T.astype(BF16)
            if then is not None:
                then(h)
            return 0

        lax.fori_loop(0, 2, step, 0)

    def backward_part(here, cols, grad_hidden):
        g, u = gate_act[here, cols], up_act[here, cols]
        sig = jax.nn.sigmoid(g)
        grad_gate = grad_hidden * u * sig * (1.0 + g * (1.0 - sig))
        grad_up = grad_hidden * (g * sig)
        acts[GATE, here, cols] = grad_gate.astype(BF16)
        acts[UP, here, cols] = grad_up.astype(BF16)
        acts_t[GATE, cols, here] = grad_gate.T.astype(BF16)
        acts_t[UP, cols, here] = grad_up.T.astype(BF16)

    def backward(first, count):
        here = pl.ds(first, count)

        def step(h, _):
            cols = pl.ds(pl.multiple_of(h * half, half), half)
            backward_part(here, cols, dot_nt(cot[here], weight_down[cols]))
            return 0

        lax.fori_loop(0, 2, step, 0)

    def met_slab(by):
        def step(h, _):
            cols = pl.ds(pl.multiple_of(h * half, half), half)
            term = dot_nt(cot[met, slab(by)], weight_down[cols, slab(by)])
            grad_hidden[:, cols] = term if by == need[0] else grad_hidden[:, cols] + term
            return 0

        lax.fori_loop(0, 2, step, 0)

    def backward_met():
        def step(h, _):
            cols = pl.ds(pl.multiple_of(h * half, half), half)
            backward_part(met, cols, grad_hidden[:, cols])
            return 0

        lax.fori_loop(0, 2, step, 0)

    def chunk(c):
        return pl.ds(pl.multiple_of(c * piece, piece), piece)

    def out_chunk(first, count, c):
        return jnp.dot(
            acts[DOWN, pl.ds(first, count)], weight_down[:, chunk(c)], preferred_element_type=F32
        )

    def grad_chunk(first, count, c):
        here = pl.ds(first, count)
        return dot_nt(acts[GATE, here], weight_in[GATE, chunk(c)]) + dot_nt(
            acts[UP, here], weight_in[UP, chunk(c)]
        )

    def return_out(first, count):
        def step(c, _):
            back_out[pl.ds(first, count), chunk(c)] = out_chunk(rows + first, count, c).astype(BF16)
            return 0

        lax.fori_loop(0, 8, step, 0)

    def return_grad():
        for i in range(4):

            def step(c, _):
                back_grad[:, chunk(c)] = grad_chunk(rows, rows, c).astype(BF16)
                return 0

            lax.fori_loop(2 * i, 2 * i + 2, step, 0)
            send_grad[i].start()

    def both_grads():
        def step(c, _):
            g = grad_chunk(0, 2 * rows, c)
            scaled[:, chunk(c)] = g[:rows]
            back_grad[:, chunk(c)] = g[rows:].astype(BF16)
            return 0

        lax.fori_loop(0, 8, step, 0)
        for copy in send_grad:
            copy.start()

    store_out = pltpu.make_async_copy(ret_out, layer_out, store_sem.at[0])
    store_grad = pltpu.make_async_copy(ret_grad, input_grad, store_sem.at[1])

    def finish_out():
        for copy in send_out:
            copy.wait_recv()

        def step(c, _):
            at = chunk(c)
            total = tok[:, at].astype(F32) + out_chunk(0, rows, c) + ret_out[:, at].astype(F32)
            ret_out[:, at] = total.astype(BF16)
            return 0

        lax.fori_loop(0, 8, step, 0)
        store_out.start()

    def own_grad():
        def step(c, _):
            scaled[:, chunk(c)] = grad_chunk(0, rows, c)
            return 0

        lax.fori_loop(0, 8, step, 0)

    def finish_grad():
        for copy in send_grad:
            copy.wait_recv()

        def grad_step(c, mixed):
            at = chunk(c)
            g = (scaled[:, at] + ret_grad[:, at].astype(F32)) * gain[:, at]
            scaled[:, at] = g
            return mixed + jnp.sum(g * tok[:, at].astype(F32), axis=1, keepdims=True)

        mixed = lax.fori_loop(0, 8, grad_step, jnp.zeros((rows, 1), F32))
        inv = inverse[:, :1]
        weight = inv * inv * inv * (mixed / depth)

        def last_step(c, _):
            at = chunk(c)
            total = cot[own, at].astype(F32) + inv * scaled[:, at]
            total = total - tok[:, at].astype(F32) * weight
            ret_grad[:, at] = total.astype(BF16)
            return 0

        lax.fori_loop(0, 8, last_step, 0)
        store_grad.start()

    whole = pl.ds(0, ff)

    def half_rows(h):
        return pl.ds(pl.multiple_of(h * half, half), half)

    def into(ref):
        def put(at, acc):
            ref[:, at] = acc.astype(BF16)

        return put

    def down_tile(to_plane, to_x, put, adds, part=whole):
        first = (to_plane * 2 + to_x) * piece
        for c in range(2):
            at = pl.ds(c * (piece // 2), piece // 2)
            cols = pl.ds(pl.multiple_of(first + c * (piece // 2), piece // 2), piece // 2)
            acc = jnp.dot(acts_t[DOWN, part], cot[:, cols], preferred_element_type=F32)
            for ref in adds:
                acc = acc + ref[:, at].astype(F32)
            put(at, acc)

    def in_tile(m, to_plane):
        cols = pl.ds(pl.multiple_of((to_plane * 2 + xl) * piece, piece), piece)
        acc = jnp.dot(acts_t[m], normed[:, cols], preferred_element_type=F32)
        return acc + jnp.dot(far_acts[m], far_normed[to_plane], preferred_element_type=F32)

    def two(step):
        def run(i, _):
            step(i)
            return 0

        lax.fori_loop(0, 2, run, 0)

    def copy_a1(way, h):
        at = half_rows(h)
        return remote(a1_out.at[way, at], a1_in.at[way, at], a1_sem.at[way, h], neighbour(way))

    def copy_a2(way, merged):
        src = a1_in.at[way] if merged else a2_out.at[way]
        return remote(src, a2_in.at[way, merged], a2_sem.at[way, merged], neighbour(way))

    copy_ax = remote(a2_in.at[0, xl], ax_in, ax_sem, partner)

    def a_opposite(h):
        at = half_rows(h)

        def send(way):
            down_tile(plane(2), way, into(a1_out.at[way, at]), (), at)
            copy_a1(way, h).start()

        two(send)

    def a_direct(way):
        down_tile(plane(1 + 2 * way), 1 - way, into(a2_out.at[way]), ())
        copy_a2(way, 0).start()

    def a_merged(way):
        copy_a1(way, 0).wait_recv()
        copy_a1(way, 1).wait_recv()
        here = a1_in.at[way]
        down_tile(plane(1 + 2 * way), way, into(here), (here,))
        copy_a2(way, 1).start()

    def a_cross():
        for way in range(2):
            for merged in range(2):
                copy_a2(way, merged).wait_recv()
        here = a2_in.at[0, xl]
        down_tile(z, 1 - xl, into(here), (here, a2_in.at[1, 1 - xl]))
        copy_ax.start()

    def store(m, out):
        copy = pltpu.make_async_copy(result.at[m], out, store_sem.at[2 + m])
        copy.start()
        return copy

    def a_last():
        copy_ax.wait_recv()

        def put(at, acc):
            result[DOWN, :, at] = (acc * factor).astype(BF16)

        down_tile(z, xl, put, (a2_in.at[0, 1 - xl], a2_in.at[1, xl], ax_in))
        return store(DOWN, down_grad)

    def far_columns(zz):
        return pl.ds(pl.multiple_of((zz * 2 + 1 - xl) * piece, piece), piece)

    def copy_near(zz):
        return remote(
            normed.at[own, far_columns(zz)], far_normed.at[zz, own], near_sem.at[zz], partner
        )

    def start_near(k):
        copy_near(plane(need[k])).start()

    def pass_on(k):
        copy_near(plane(need[k])).wait_recv()
        copy_pass(plane(need[k])).start()

    def copy_rest(zz):
        return remote(
            normed.at[met, far_columns(zz)], far_normed.at[zz, met], rest_sem.at[zz], partner
        )

    def copy_pass(zz):
        return pltpu.make_async_remote_copy(
            src_ref=far_normed.at[zz, own],
            dst_ref=far_normed.at[zz, met],
            send_sem=pass_sem.at[zz],
            recv_sem=rest_sem.at[zz, 1],
            device_id=to_before,
            device_id_type=MESH,
        )

    def copy_far(m):
        return remote(acts_t.at[m], far_acts.at[m], far_sem.at[m], partner)

    def copy_b1(m, way):
        return remote(
            bo_out.at[m, half_rows(way)], b1_in.at[m, way], b1_sem.at[m, way], neighbour(way)
        )

    def copy_b2(m, way, merged):
        src = b1_in.at[m, way] if merged else bd_out.at[m, way]
        return remote(src, b2_in.at[m, way, merged], b2_sem.at[m, way, merged], neighbour(way))

    own_tile = (gate_act, up_act)

    def arrived(by):
        @pl.when(core == 0)
        def _():
            copy_near(plane(by)).wait_recv()

        copy_rest(plane(by)).wait_recv()

    def b_first(m):
        copy_far(m).wait_recv()
        if m == GATE:
            arrived(2)
        bo_out[m] = in_tile(m, plane(2)).astype(BF16)
        for way in range(2):
            copy_b1(m, way).start()
        for way in range(2):
            if m == GATE:
                arrived(1 + 2 * way)
            tile = in_tile(m, plane(1 + 2 * way))
            straight, later = (tile[half:], tile[:half]) if way == 0 else (tile[:half], tile[half:])
            bd_out[m, way] = straight.astype(BF16)
            copy_b2(m, way, 0).start()
            held[m, way] = later

    def b_own():
        arrived(0)
        for m in (GATE, UP):
            own_tile[m][...] = in_tile(m, z)

    def b_merged(m):
        for way in range(2):
            copy_b1(m, way).wait_recv()
            b1_in[m, way] = (held[m, way] + b1_in[m, way].astype(F32)).astype(BF16)
            copy_b2(m, way, 1).start()

    def b_last(m, out):
        for way in range(2):
            for merged in range(2):
                copy_b2(m, way, merged).wait_recv()
        for h in range(2):
            at = pl.ds(h * half, half)
            total = own_tile[m][at] + b2_in[m, 0, 1 - h].astype(F32) + b2_in[m, 1, h].astype(F32)
            result[m, at] = (total * factor).astype(BF16)
        return store(m, out)

    for copy in load_rows:
        copy.wait()
    for copy in load_rest:
        copy.start()
    normalize(tok, 0, rows, True)
    start_near(0)
    start_near(1)

    @pl.when(core == 0)
    def _():
        forward(0, rows, True)
        for copy in send_tok:
            copy.wait_recv()
        normalize(normed, rows, rows, False)
        for copy in load_rest:
            copy.wait()
        send_cot[0].wait_recv()
        forward(rows, rows, then=a_opposite)
        for copy in send_cot[1:]:
            copy.wait_recv()
        backward(0, 2 * rows)
        copy_far(GATE).start()
        two(a_direct)
        start_near(2)
        copy_far(UP).start()
        two(a_merged)
        start_near(3)
        return_out(0, rows)
        for copy in send_out:
            copy.start()
        both_grads()

    @pl.when(core == 1)
    def _():
        forward(0, rows, True)
        for copy in load_rest:
            copy.wait()
        backward(0, rows)
        own_grad()
        pass_on(0)
        pass_on(1)
        start_near(2)
        for i in range(2):
            send_tok[i].wait_recv()
            start_near(3) if i == 0 else pass_on(2)
            normalize(normed, rows + i * part, part, False)
            forward(rows + i * part, part)
            return_out(i * part, part)
            send_out[i].start()
        pass_on(3)
        for by in need:
            copy_rest(plane(by)).start()
        send_cot[0].wait_recv()
        two(a_opposite)
        met_slab(2)
        finish_out()
        finish_grad()
        send_cot[1].wait_recv()
        a_direct(0)
        met_slab(1)
        send_cot[2].wait_recv()
        a_direct(1)
        met_slab(3)
        two(a_merged)
        send_cot[3].wait_recv()
        met_slab(0)
        backward_met()
        copy_far(GATE).start()
        copy_far(UP).start()
        return_grad()

    b_first(GATE)
    b_first(UP)

    @pl.when(core == 1)
    def _():
        a_cross()
        b_own()

    b_merged(GATE)
    b_merged(UP)

    @pl.when(core == 0)
    def _():
        a_cross()
        b_own()
        finish_out()

    stores = [a_last()]
    stores.append(b_last(GATE, gate_grad))
    stores.append(b_last(UP, up_grad))

    @pl.when(core == 0)
    def _():
        finish_grad()

    for copy in stores:
        copy.wait()
    store_out.wait()
    store_grad.wait()
    for copy in (*send_tok, *send_cot, *send_out, *send_grad, copy_ax):
        copy.wait_send()

    for zz in range(4):
        copy_near(zz).wait_send()

    @pl.when(core == 1)
    def _():
        for zz in range(4):
            copy_rest(zz).wait_send()
            copy_pass(zz).wait_send()

    for i in range(2):
        copy_a1(i, 0).wait_send()
        copy_a1(i, 1).wait_send()
        copy_far(i).wait_send()
        for k in range(2):
            copy_a2(i, k).wait_send()
            copy_b1(i, k).wait_send()
            copy_b2(i, k, 0).wait_send()
            copy_b2(i, k, 1).wait_send()


def write_out(
    layer_in,
    input_in,
    gate_in,
    up_in,
    down_in,
    layer_out,
    input_grad,
    gate_grad,
    up_grad,
    down_grad,
    rows,
    near,
    far,
    sems,
):
    pieces = 4
    count = layer_in.shape[0] // pieces
    moves = []
    for k, (src, dst) in enumerate(((layer_in, layer_out), (input_in, input_grad))):
        for i in range(pieces):
            at, sem = pl.ds(i * count, count), 3 + k * pieces + i
            moves.append(
                (
                    pltpu.make_async_copy(src.at[at], rows.at[k, at], sems.at[0, sem]),
                    pltpu.make_async_copy(rows.at[k, at], dst.at[at], sems.at[1, sem]),
                )
            )
    grads = [
        (
            pltpu.make_async_copy(src, near.at[m], sems.at[0, m]),
            pltpu.make_async_copy(far.at[m], dst, sems.at[1, m]),
        )
        for m, (src, dst) in enumerate(
            ((gate_in, gate_grad), (up_in, up_grad), (down_in, down_grad))
        )
    ]
    for load, _ in grads + moves:
        load.start()
    for m, (load, store) in enumerate(grads):
        load.wait()
        if m == DOWN:
            far[m] = near[m].astype(F32)
        else:
            far[m] = near[m].T.astype(F32)
        store.start()
    for load, store in moves:
        load.wait()
        store.start()
    for _, store in grads + moves:
        store.wait()


def body(sections, tokens, norm_gain, gate_weight, up_weight, down_weight, cotangent):
    rows, depth = tokens.shape
    ff = down_weight.shape[0]
    half = ff // 2
    piece = depth // 8
    anywhere = pl.BlockSpec(memory_space=pl.ANY)
    dma = pltpu.SemaphoreType.DMA

    def vmem(*shape, dtype=BF16):
        return pltpu.VMEM(shape, dtype)

    flops = 2 * 18 * rows * depth * ff
    parts = pl.pallas_call(
        functools.partial(kernel, sections),
        out_shape=(
            jax.ShapeDtypeStruct((rows, depth), BF16),
            jax.ShapeDtypeStruct((rows, depth), BF16),
            jax.ShapeDtypeStruct((ff, piece), BF16),
            jax.ShapeDtypeStruct((ff, piece), BF16),
            jax.ShapeDtypeStruct((ff, piece), BF16),
        ),
        in_specs=[anywhere] * 6,
        out_specs=(anywhere,) * 5,
        scratch_shapes=[
            vmem(1, depth, dtype=F32),
            vmem(2, depth, ff),
            vmem(ff, depth),
            vmem(rows, depth),
            vmem(2 * rows, depth),
            vmem(2 * rows, depth),
            vmem(rows, 128, dtype=F32),
            vmem(2 * rows, ff, dtype=F32),
            vmem(2 * rows, ff, dtype=F32),
            vmem(rows, ff, dtype=F32),
            vmem(3, 2 * rows, ff),
            vmem(3, ff, 2 * rows),
            vmem(rows, depth, dtype=F32),
            vmem(rows, depth),
            vmem(rows, depth),
            vmem(rows, depth),
            vmem(rows, depth),
            vmem(2, ff, piece),
            vmem(2, ff, piece),
            vmem(2, ff, piece),
            vmem(2, 2, ff, piece),
            vmem(ff, piece),
            vmem(4, 2 * rows, piece),
            vmem(2, ff, 2 * rows),
            vmem(2, ff, piece),
            vmem(2, 2, half, piece),
            vmem(2, 2, half, piece, dtype=F32),
            vmem(2, 2, half, piece),
            vmem(2, 2, 2, half, piece),
            vmem(3, ff, piece),
            dma((8,)),
            dma((5,)),
            dma((6, 2)),
            dma((6, 2)),
            dma((2, 2, 2)),
            dma((2, 2, 2)),
            dma((2,)),
            dma((4, 2)),
            dma((4, 2)),
            dma((4,)),
            dma((2, 2)),
            dma((2, 2, 2)),
            dma((2, 2, 2, 2)),
        ],
        compiler_params=pltpu.CompilerParams(
            collective_id=0, has_side_effects=True, vmem_limit_bytes=63 * 2**20
        ),
        cost_estimate=pl.CostEstimate(
            flops=flops, bytes_accessed=23 * 2**20, transcendentals=4 * rows * ff
        ),
    )(tokens, norm_gain.reshape(1, depth), gate_weight, up_weight, down_weight, cotangent)
    return pl.pallas_call(
        write_out,
        out_shape=(
            jax.ShapeDtypeStruct((rows, depth), BF16),
            jax.ShapeDtypeStruct((rows, depth), BF16),
            jax.ShapeDtypeStruct((piece, ff), F32),
            jax.ShapeDtypeStruct((piece, ff), F32),
            jax.ShapeDtypeStruct((ff, piece), F32),
        ),
        in_specs=[anywhere] * 5,
        out_specs=(anywhere,) * 5,
        scratch_shapes=[
            vmem(2, rows, depth),
            vmem(3, ff, piece),
            vmem(3, ff, piece, dtype=F32),
            dma((2, 11)),
        ],
        compiler_params=pltpu.CompilerParams(vmem_limit_bytes=63 * 2**20),
        cost_estimate=pl.CostEstimate(flops=0, bytes_accessed=13 * 2**20, transcendentals=0),
    )(*parts)


def solution(mesh):
    in_specs = (
        P(("section", "dp"), None),
        P(),
        P(None, "section"),
        P(None, "section"),
        P("section", None),
        P(("section", "dp"), None),
    )
    out_specs = (
        P(("section", "dp"), None),
        P(("section", "dp"), None),
        P("dp", "section"),
        P("dp", "section"),
        P("section", "dp"),
    )
    return jax.shard_map(
        functools.partial(body, mesh.shape["section"]),
        mesh=mesh,
        in_specs=in_specs,
        out_specs=out_specs,
        check_vma=False,
    )
```
